512 devices in a mesh: fsdp: 8 (over y_lo, x), wide: 64 (over y_hi, z, core).
Axes of the slice: x: 4, y: 8 (y_hi: 4, y_lo: 2; y = y_hi * 2 + y_lo), z: 8, core: 2. Of those that a mesh axis runs over, the one named last changes fastest.
Arguments:
- patches: bfloat16 [131072, 1280], P(('fsdp', 'wide')), may hold values from -6 to 6
- ln_gain: float32 [1280], replicated, may hold values from 0.1 to 1.9
- qkv_weight: bfloat16 [1280, 3840], P(None, 'fsdp')
- proj_weight: bfloat16 [1280, 1280], P('fsdp'), may hold values from -0.15625 to 0.15625
- out_cotangent: bfloat16 [131072, 1280], P(('fsdp', 'wide')), may hold values from -0.0625 to 0.0625
- tile_counts: int32 [512], P(('fsdp', 'wide')), may hold values from 1 to 2, as said below
- segment_ids: int32 [131072], P(('fsdp', 'wide')), may hold values from 0 to 63, as said below
Outputs:
- output: bfloat16 [131072, 1280], P(('fsdp', 'wide'))
- proj_grad: bfloat16 [1280, 1280], P('fsdp')
The draws below stay inside these ranges and needn't reach their ends.
Inputs may be any that keep to these rules, and one draw needn't show every extreme that they name: Each device's live patches are its first tile_counts times 128 slots; some device is full and some holds one tile. `segment_ids`: within one device's slots the image number never falls, changes only at multiples of 4 slots, rises by at most one there and starts at 0; some device reaches the largest value.
All inputs are finite; a program needn't handle non-finite values.
Results may differ from the reference program's by a relative error of at most 0.035.
Values may be sent and summed in bfloat16 or wider, within the bound.
No kernel may reach another device: no remote copies, remote signals or barrier semaphores. Data moves between devices by JAX's collectives and lax.ppermute only.
A program may use at most 64 MiB of HBM per device.

```python
import jax
import jax.numpy as jnp
from jax import lax

D = 1280
HEADS = 16
HEAD = 80
TILE = 128
MAXT = 2
ROWS_DEV = 256
TOKENS = 131072


def draw_qkv_weight(key, part):
    key = jax.random.fold_in(key, 1)
    drawn = jax.random.normal(key, (D, 3 * D), jnp.float32) * D ** (-0.5)
    return drawn.astype(jnp.bfloat16)


def draw_tile_counts(key, part):
    key = jax.random.fold_in(key, 4)
    device_count = TOKENS // ROWS_DEV
    drawn = jax.random.randint(key, (device_count,), 1, MAXT + 1)
    chosen = jax.random.randint(jax.random.fold_in(key, 5), (), 0, device_count)
    drawn = drawn.at[chosen].set(MAXT)
    drawn = drawn.at[(chosen + 1) % device_count].set(1)
    return drawn.astype(jnp.int32)


def draw_segment_ids(key, part):
    key = jax.random.fold_in(key, 6)
    device_count = TOKENS // ROWS_DEV
    groups = ROWS_DEV // 4
    starts = (jax.random.randint(key, (device_count, groups), 0, 20) == 0).astype(jnp.int32)
    busiest = jax.random.randint(jax.random.fold_in(key, 7), (), 0, device_count)
    starts = jnp.where((jnp.arange(device_count) == busiest)[:, None], jnp.ones_like(starts), starts)
    starts = starts.at[:, 0].set(0)
    labels = jnp.cumsum(starts, axis=1)
    return jnp.repeat(labels, 4, axis=1).reshape(TOKENS).astype(jnp.int32)


def strengthened(values, own_key, source, target, parts, factor):
    def block_of(axis_at):
        return (jnp.arange(values.shape[axis_at]) // (values.shape[axis_at] // parts)).reshape((-1,) + (1,) * (values.ndim - 1 - axis_at))

    near = jax.random.permutation(own_key, parts)[block_of(target)]
    other_side = (block_of(target) + parts // 2) % parts
    return jnp.where((block_of(source) == near) | (block_of(source) == other_side), factor * values, values)


def shard_levels(stream_key, shape, cuts, low, high):
    level, own = 1.0, jax.random.fold_in(stream_key, 6)
    for axis_at, parts in cuts:
        steps = jnp.exp(jax.random.uniform(jax.random.fold_in(own, axis_at), (parts,), jnp.float32, low / len(cuts), high / len(cuts)))
        level = level * jnp.repeat(steps, shape[axis_at] // parts).reshape([-1 if axis == axis_at else 1 for axis in range(len(shape))])
    return level


def bell_draw(stream_key, extent, deviation, limit, cuts=(), held_as=jnp.bfloat16):
    gain = shard_levels(stream_key, extent, cuts, -0.22, 0.18) if cuts else 1.0
    result = jax.random.normal(stream_key, extent, jnp.float32) * deviation * gain
    return jnp.minimum(jnp.maximum(result, -limit), limit).astype(held_as)


def heavy_noise(stream_key, dims, spread, limit, shards, heavy, kind=jnp.bfloat16):
    result = spread * jax.random.normal(stream_key, dims, jnp.float32)
    if shards:
        result = result * shard_levels(stream_key, dims, shards, -0.22, 0.18)
    return jnp.clip(strengthened(result, jax.random.fold_in(stream_key, 3), *heavy), -limit, limit).astype(kind)


def setup_inputs(seed: int = 0) -> dict:
    seeds = jax.random.split(jax.random.key(seed), 8)
    return {
        "patches": bell_draw(seeds[0], (TOKENS, D), 1.0, 6.0, ((0, 512),)),
        "ln_gain": jnp.clip(1.0 + 0.18 * jax.random.normal(seeds[1], (D,), jnp.float32), 0.1, 1.9),
        "qkv_weight": draw_qkv_weight(jax.random.fold_in(seeds[7], 71), 0),
        "proj_weight": bell_draw(seeds[3], (D, D), D ** -0.5, 0.15625, ((0, 8),)),
        "out_cotangent": heavy_noise(seeds[4], (TOKENS, D), (TOKENS ** -0.5), 0.0625, ((0, 512),), (0, 1, 256, 6.0)),
        "tile_counts": draw_tile_counts(jax.random.fold_in(seeds[7], 71), 0),
        "segment_ids": draw_segment_ids(jax.random.fold_in(seeds[7], 71), 0),
    }


epsilon = 1e-06

def one_device(patches, ln_gain, qkv_weight, proj_weight, out_cotangent, count, images):
    row_count = patches.shape[0]
    alive = jnp.arange(row_count, dtype=jnp.int32) < count * TILE
    inputs = patches.astype(jnp.float32)
    row_mean = lax.optimization_barrier(jnp.mean(inputs, axis=1, keepdims=True))
    centred = inputs - row_mean
    variance = lax.optimization_barrier(jnp.mean(centred * centred, axis=1, keepdims=True))
    normed = (centred * lax.rsqrt(variance + epsilon) * ln_gain).astype(jnp.bfloat16)
    mixed = jnp.dot(normed, qkv_weight, preferred_element_type=jnp.float32).astype(jnp.bfloat16)
    queries = mixed[:, :D].reshape(row_count, HEADS, HEAD).astype(jnp.float32)
    keyset = mixed[:, D:2 * D].reshape(row_count, HEADS, HEAD).astype(jnp.float32)
    valueset = mixed[:, 2 * D:].reshape(row_count, HEADS, HEAD).astype(jnp.float32)
    scores = jnp.einsum('qhd,khd->hqk', queries, keyset) * HEAD ** (-0.5)
    allowed = (images[:, None] == images[None, :]) & (alive[:, None] == alive[None, :])
    scores = jnp.where(allowed[None], scores, jnp.float32(-1e+30))
    peak = lax.optimization_barrier(jnp.max(scores, axis=2, keepdims=True))
    weights = jnp.exp(scores - peak)
    probs = (weights / lax.optimization_barrier(jnp.sum(weights, axis=2, keepdims=True))).astype(jnp.bfloat16)
    context = jnp.einsum('hqk,khd->qhd', probs.astype(jnp.float32), valueset).reshape(row_count, D)
    context = jnp.where(alive[:, None], context, jnp.float32(0.0)).astype(jnp.bfloat16)
    projected = jnp.dot(context, proj_weight, preferred_element_type=jnp.float32)
    output = jnp.where(alive[:, None], inputs + projected, jnp.float32(0.0)).astype(jnp.bfloat16)
    cotangent = jnp.where(alive[:, None], out_cotangent, jnp.zeros_like(out_cotangent))
    partial_value = jnp.dot(context.T, cotangent, preferred_element_type=jnp.float32).astype(jnp.bfloat16)
    partial_value = lax.optimization_barrier(partial_value).astype(jnp.float32)
    return (output, partial_value)

def reference(patches, ln_gain, qkv_weight, proj_weight, out_cotangent, tile_counts, segment_ids):
    device_count = TOKENS // ROWS_DEV
    blocks = patches.reshape(device_count, ROWS_DEV, D)
    cotangents = out_cotangent.reshape(device_count, ROWS_DEV, D)
    images = segment_ids.reshape(device_count, ROWS_DEV)

    def step(total, pieces):
        block, cotangent, count, image_row = pieces
        output, partial_value = one_device(block, ln_gain, qkv_weight, proj_weight, cotangent, count, image_row)
        return (total + partial_value, output)
    total, outputs = lax.scan(step, jnp.zeros((D, D), jnp.float32), (blocks, cotangents, tile_counts, images))
    return (outputs.reshape(TOKENS, D), total.astype(jnp.bfloat16))
```

```python
import functools
import math

import jax
import jax.numpy as jnp
import numpy as np
from jax import lax
from jax.experimental import pallas as pl
from jax.experimental.pallas import tpu as pltpu
from jax.sharding import Mesh
from jax.sharding import PartitionSpec as P

HEADS = 16
HEAD = 80
TILE = 128
ROWS = 256
WIDTH = 1280
EPSILON = 1e-06
BF16 = jnp.bfloat16
F32 = jnp.float32

Y_HI, Z, CORES = 4, 8, 2

HEAD_SETS = ((1, 2, 5, 6), (0, 3, 4, 7))


def block_tables():
    sends = np.zeros((8, 2, 2), np.int32)
    orders = np.zeros((2, 16), np.int32)
    for half, heads in enumerate(HEAD_SETS):
        for shard in range(8):
            picked = [k for k in range(3) if (3 * shard + k) % 8 in heads] + ([3] if shard in heads else [])
            assert len(picked) == 2
            for place, k in enumerate(picked):
                sends[shard, half, place] = k
                if k == 3:
                    slot = 12 + heads.index(shard)
                else:
                    kind, m = divmod(3 * shard + k, 8)
                    slot = 4 * kind + heads.index(m)
                orders[half, slot] = 2 * shard + place
    return sends, orders


SENDS, ORDERS = block_tables()
OWN_HALF = np.array([1 if j in HEAD_SETS[1] else 0 for j in range(8)], np.int32)


def norm_kernel(count_ref, patches_ref, gain_ref, images_ref, message_ref):
    inputs = patches_ref[...].astype(F32)
    row_mean = jnp.mean(inputs, axis=1, keepdims=True)
    centred = inputs - row_mean
    variance = jnp.mean(centred * centred, axis=1, keepdims=True)
    message_ref[:ROWS, :] = (centred * lax.rsqrt(variance + EPSILON) * gain_ref[...]).astype(BF16)
    dead = lax.broadcasted_iota(jnp.int32, (1, ROWS), 1) >= count_ref[0] * TILE
    code = (images_ref[...] + jnp.where(dead, 64, 0)).astype(F32)
    message_ref[ROWS:, :] = jnp.zeros((16, WIDTH), BF16)
    message_ref[ROWS:, :ROWS] = jnp.broadcast_to(code, (16, ROWS)).astype(BF16)


def attention_kernel(order_ref, x0_ref, x1_ref, x2_ref, x3_ref, blocks_ref, context_ref, weight_ref):
    scale = HEAD**-0.5 * math.log2(math.e)
    hidden = -1e30 * HEAD**0.5
    for slot in range(12):
        weight_ref[slot * HEAD : (slot + 1) * HEAD, :] = blocks_ref[order_ref[slot]]
    for part, x_ref in enumerate((x0_ref, x1_ref, x2_ref, x3_ref)):
        mixed = lax.dot_general(
            weight_ref[...], x_ref[:ROWS, :], (((1,), (1,)), ((), ())), preferred_element_type=F32
        ).astype(BF16)
        code = x_ref[ROWS : ROWS + 16, :ROWS].astype(F32)[0:1, :]
        square = jnp.broadcast_to(code, (ROWS, ROWS))
        allowed = square == square.T
        alive = code < 64.0
        for head in range(4):
            queries = mixed[head * HEAD : (head + 1) * HEAD, :]
            keyset = mixed[(4 + head) * HEAD : (5 + head) * HEAD, :]
            valueset = mixed[(8 + head) * HEAD : (9 + head) * HEAD, :]
            scores = lax.dot_general(keyset, queries, (((0,), (0,)), ((), ())), preferred_element_type=F32)
            scores = jnp.where(allowed, scores, hidden)
            peak = jnp.max(scores, axis=0, keepdims=True)
            weights = jnp.exp2((scores - peak) * scale)
            total = jnp.sum(weights, axis=0, keepdims=True)
            context = jnp.dot(valueset, weights.astype(BF16), preferred_element_type=F32)
            context = jnp.where(alive, context / total, 0.0)
            context_ref[part, head * HEAD : (head + 1) * HEAD, :] = context.astype(BF16)


def gradient_kernel(context_ref, c0_ref, c1_ref, c2_ref, c3_ref, grad_ref):
    for start in range(0, WIDTH, 256):
        total = None
        for part, c_ref in enumerate((c0_ref, c1_ref, c2_ref, c3_ref)):
            term = jnp.dot(context_ref[part], c_ref[:, start : start + 256], preferred_element_type=F32)
            total = term if total is None else total + term
        grad_ref[:, start : start + 256] = total.astype(BF16)


def project_kernel(order_ref, context_ref, blocks_ref, keep_ref, send_ref, weight_ref):
    for slot in range(4):
        weight_ref[slot * HEAD : (slot + 1) * HEAD, :] = blocks_ref[order_ref[12 + slot]]
    for part in range(4):
        projected = lax.dot_general(
            context_ref[part], weight_ref[...], (((0,), (0,)), ((), ())), preferred_element_type=F32
        )
        target = send_ref if part % 2 else keep_ref
        target[part // 2] = projected.astype(BF16)


VMEM = pl.BlockSpec(memory_space=pltpu.VMEM)
SMEM = pl.BlockSpec(memory_space=pltpu.SMEM)


def call(kernel, out_shape, in_specs, out_specs, scratch=(), limit=24 << 20, flops=0, read=0):
    return pl.pallas_call(
        kernel,
        out_shape=out_shape,
        in_specs=in_specs,
        out_specs=out_specs,
        scratch_shapes=scratch,
        compiler_params=pltpu.CompilerParams(vmem_limit_bytes=limit),
        cost_estimate=pl.CostEstimate(flops=flops, bytes_accessed=read, transcendentals=0),
    )


def array(*shape):
    return jax.ShapeDtypeStruct(shape, BF16)


def shards(patches, ln_gain, qkv_weight, proj_weight, out_cotangent, tile_counts, segment_ids):
    core = lax.axis_index("core")
    half = lax.axis_index("z") % 2
    shard = lax.axis_index("y_lo") * 4 + lax.axis_index("x")
    core_pairs = [(0, 1), (1, 0)]
    z_pairs = [(i, i ^ 1) for i in range(Z)]
    x_pairs = [(i, i ^ 1) for i in range(4)]

    def to_core(value):
        return lax.ppermute(value, "core", core_pairs)

    def to_pair(value):
        return lax.ppermute(value, "z", z_pairs)

    blocks = jnp.concatenate([qkv_weight.T.reshape(6, HEAD, WIDTH), proj_weight.reshape(2, HEAD, WIDTH)])
    sends = jnp.asarray(SENDS)[shard, half]
    own = jnp.concatenate([lax.dynamic_index_in_dim(blocks, 2 * sends[i] + core, 0) for i in range(2)])
    gathered = lax.all_to_all(
        jnp.broadcast_to(own[None], (8, 2, HEAD, WIDTH)), ("y_lo", "x"), 0, 0
    ).reshape(16, HEAD, WIDTH)
    order = jnp.asarray(ORDERS)[half]

    message = call(
        norm_kernel, array(ROWS + 16, WIDTH), [SMEM, VMEM, VMEM, VMEM], VMEM, read=3 * ROWS * WIDTH
    )(tile_counts, patches, ln_gain.reshape(1, WIDTH), segment_ids.reshape(1, ROWS))
    message_pair = to_pair(message)
    message_core = to_core(message)
    message_both = to_core(message_pair)

    cotangent_pair = to_pair(out_cotangent)
    cotangent_core = to_core(out_cotangent)
    cotangent_both = to_core(cotangent_pair)

    context = call(
        attention_kernel,
        array(4, 4 * HEAD, ROWS),
        [SMEM] + [VMEM] * 5,
        VMEM,
        [pltpu.VMEM((12 * HEAD, WIDTH), BF16)],
        flops=2 * 1024 * 1280 * 960 + 4 * 16 * 256 * 256 * 128,
        read=8 << 20,
    )(order, message, message_core, message_pair, message_both, gathered)

    grad = call(
        gradient_kernel, array(4 * HEAD, WIDTH), [VMEM] * 5, VMEM, flops=2 * 1024 * 1280 * 320, read=4 << 20
    )(context, out_cotangent, cotangent_core, cotangent_pair, cotangent_both)
    grad = lax.all_to_all(grad.reshape(8, 40, WIDTH), ("y_lo", "x"), 0, 0)
    grad = jnp.sum(grad.astype(F32), axis=0).astype(BF16)
    grad = lax.all_to_all(jnp.broadcast_to(grad[None], (Y_HI, 40, WIDTH)), "y_hi", 0, 0)
    grad = jnp.sum(grad.astype(F32), axis=0).astype(BF16)
    grad = lax.all_to_all(jnp.broadcast_to(grad[None], (Z, 40, WIDTH)), "z", 0, 0)
    grad = jnp.sum(grad.astype(F32).reshape(Z // 2, 2, 40, WIDTH), axis=0).astype(BF16)
    mine = jnp.asarray(OWN_HALF)[shard] == 1
    keep = jnp.where(mine, grad[1], grad[0])
    got = lax.ppermute(jnp.where(mine, grad[0], grad[1]), "x", x_pairs)
    even = shard % 2 == 0
    head_grad = jnp.concatenate([jnp.where(even, keep, got), jnp.where(even, got, keep)])
    other_grad = to_core(head_grad)
    first = core == 0
    proj_grad = jnp.concatenate([jnp.where(first, head_grad, other_grad), jnp.where(first, other_grad, head_grad)])

    keep_out, send_out = call(
        project_kernel,
        (array(2, ROWS, WIDTH), array(2, ROWS, WIDTH)),
        [SMEM, VMEM, VMEM],
        (VMEM, VMEM),
        [pltpu.VMEM((4 * HEAD, WIDTH), BF16)],
        flops=2 * 1024 * 1280 * 320,
        read=6 << 20,
    )(order, context, gathered)
    from_core = to_core(send_out)
    from_pair = to_pair((keep_out[1].astype(F32) + from_core[1].astype(F32)).astype(BF16))
    projected = keep_out[0].astype(F32) + from_core[0].astype(F32) + from_pair.astype(F32)
    alive = lax.iota(jnp.int32, ROWS) < tile_counts[0] * TILE
    output = jnp.where(alive[:, None], patches.astype(F32) + projected, F32(0.0)).astype(BF16)
    return output, proj_grad


def solution(mesh):
    fine = Mesh(mesh.devices.reshape(2, 4, Y_HI, Z, CORES), ("y_lo", "x", "y_hi", "z", "core"))
    fsdp = ("y_lo", "x")
    every = ("y_lo", "x", "y_hi", "z", "core")
    return jax.shard_map(
        shards,
        mesh=fine,
        in_specs=(P(every, None), P(), P(None, fsdp), P(fsdp, None), P(every, None), P(every), P(every)),
        out_specs=(P(every, None), P(fsdp, None)),
        check_vma=False,
    )
```

```python
import math

import jax
import jax.numpy as jnp
import numpy as np
from jax import lax
from jax.experimental import pallas as pl
from jax.experimental.pallas import tpu as pltpu
from jax.sharding import Mesh
from jax.sharding import PartitionSpec as P

HEADS = 16
HEAD = 80
TILE = 128
ROWS = 256
NOTE = 16
WIDTH = 1280
EPSILON = 1e-06
BF16 = jnp.bfloat16
F32 = jnp.float32

Y_HI, Z_QUAD, Z_PAIR, CORES = 4, 4, 2, 2
AXES = ("y_lo", "x", "y_hi", "z_quad", "z_pair", "core")
FSDP = ("y_lo", "x")

HEAD_SETS = ((1, 2, 5, 6), (0, 3, 4, 7))


def block_tables():
    sends = np.zeros((8, 2, 2), np.int32)
    orders = np.zeros((2, 16), np.int32)
    for half, heads in enumerate(HEAD_SETS):
        for shard in range(8):
            picked = [k for k in range(3) if (3 * shard + k) % 8 in heads] + ([3] if shard in heads else [])
            assert len(picked) == 2
            for place, k in enumerate(picked):
                sends[shard, half, place] = k
                if k == 3:
                    slot = 12 + heads.index(shard)
                else:
                    kind, m = divmod(3 * shard + k, 8)
                    slot = 4 * kind + heads.index(m)
                orders[half, slot] = 2 * shard + place
    return sends.reshape(-1), orders.reshape(-1)


SENDS, ORDERS = block_tables()


def owns(x, half):
    return int(x in (0, 3)) == half


CORE_SWAP = [(0, 1), (1, 0)]
PAIR_SWAP = [(0, 1), (1, 0)]
TO_OWNER = [
    (2 * x + half, 2 * x + (1 - half) if owns(x, half) else 2 * (x ^ 1) + half) for x in range(4) for half in range(2)
]
ACROSS = [(2 * x + half, 2 * (x ^ 1) + (1 - half)) for x in range(4) for half in range(2) if not owns(x, half)]


def front_kernel(
    place_ref,
    sends_ref,
    count_ref,
    patches_ref,
    gain_ref,
    images_ref,
    qkv_ref,
    proj_ref,
    out_ref,
    blocks_ref,
    rows_ref,
    message_ref,
    held_ref,
    read_sems,
    write_sems,
    sems,
):
    fetch = pltpu.make_async_copy(patches_ref, rows_ref, sems.at[0])
    fetch.start()
    core = place_ref[1]
    for i in range(2):
        choice = sends_ref[2 * place_ref[0] + i]

        @pl.when(choice < 3)
        def _():
            pltpu.make_async_copy(qkv_ref.at[2 * jnp.minimum(choice, 2) + core], held_ref.at[i], read_sems.at[i]).start()

        @pl.when(choice == 3)
        def _():
            pltpu.make_async_copy(proj_ref.at[core], held_ref.at[i], read_sems.at[i]).start()

    copies = []
    for i in range(2):
        pltpu.make_async_copy(proj_ref.at[0], held_ref.at[i], read_sems.at[i]).wait()
        for peer in range(8):
            copies.append(pltpu.make_async_copy(held_ref.at[i], blocks_ref.at[peer, i], write_sems.at[8 * i + peer]))
            copies[-1].start()

    fetch.wait()
    inputs = rows_ref[...].astype(F32)
    row_mean = jnp.mean(inputs, axis=1, keepdims=True)
    centred = inputs - row_mean
    variance = jnp.mean(centred * centred, axis=1, keepdims=True)
    message_ref[:ROWS, :] = (centred * lax.rsqrt(variance + EPSILON) * gain_ref[...].reshape(1, WIDTH)).astype(BF16)
    dead = lax.broadcasted_iota(jnp.int32, (1, ROWS), 1) >= count_ref[0] * TILE
    code = (images_ref[...].reshape(1, ROWS) + jnp.where(dead, 64, 0)).astype(F32)
    message_ref[ROWS:, :] = jnp.zeros((NOTE, WIDTH), BF16)
    message_ref[ROWS:, :ROWS] = jnp.broadcast_to(code, (NOTE, ROWS)).astype(BF16)
    copies.append(pltpu.make_async_copy(message_ref, out_ref, sems.at[1]))
    copies[-1].start()
    for copy in copies:
        copy.wait()


def attention_kernel(
    place_ref,
    order_ref,
    x0_ref,
    x1_ref,
    x2_ref,
    x3_ref,
    blocks_ref,
    out_ref,
    x_ref,
    weight_ref,
    context_ref,
    x_sems,
    sems,
    out_sem,
):
    scale = HEAD**-0.5 * math.log2(math.e)
    hidden = -1e30 * HEAD**0.5
    copies = []
    for slot in range(12):
        source = blocks_ref.at[order_ref[16 * place_ref[2] + slot]]
        copies.append(pltpu.make_async_copy(source, weight_ref.at[slot * HEAD : (slot + 1) * HEAD], sems.at[slot]))
    arrivals = [
        pltpu.make_async_copy(ref, x_ref.at[part], x_sems.at[part])
        for part, ref in enumerate((x0_ref, x1_ref, x2_ref, x3_ref))
    ]
    for copy in copies + arrivals:
        copy.start()
    for copy in copies + arrivals:
        copy.wait()
    for part in range(4):
        mixed = lax.dot_general(
            weight_ref[...], x_ref[part, :ROWS, :], (((1,), (1,)), ((), ())), preferred_element_type=F32
        ).astype(BF16)
        code = x_ref[part, ROWS:, :ROWS].astype(F32)[0:1, :]
        square = jnp.broadcast_to(code, (ROWS, ROWS))
        allowed = square == square.T
        alive = code < 64.0
        for head in range(4):
            queries = mixed[head * HEAD : (head + 1) * HEAD, :]
            keyset = mixed[(4 + head) * HEAD : (5 + head) * HEAD, :]
            valueset = mixed[(8 + head) * HEAD : (9 + head) * HEAD, :]
            scores = lax.dot_general(keyset, queries, (((0,), (0,)), ((), ())), preferred_element_type=F32)
            scores = jnp.where(allowed, scores, hidden)
            peak = jnp.max(scores, axis=0, keepdims=True)
            weights = jnp.exp2((scores - peak) * scale)
            total = jnp.sum(weights, axis=0, keepdims=True)
            context = jnp.dot(valueset, weights.astype(BF16), preferred_element_type=F32)
            context = jnp.where(alive, context / total, 0.0)
            context_ref[head * HEAD : (head + 1) * HEAD, part * ROWS : (part + 1) * ROWS] = context.astype(BF16)
    store = pltpu.make_async_copy(context_ref, out_ref, out_sem)
    store.start()
    store.wait()


def gradient_kernel(from_ref, c0_ref, c1_ref, c2_ref, c3_ref, grad_ref, context_ref, c_ref, sems):
    copies = [
        pltpu.make_async_copy(ref, c_ref.at[part * ROWS : (part + 1) * ROWS], sems.at[part])
        for part, ref in enumerate((c0_ref, c1_ref, c2_ref, c3_ref))
    ]
    copies.append(pltpu.make_async_copy(from_ref, context_ref, sems.at[4]))
    for copy in copies:
        copy.start()
    for copy in copies:
        copy.wait()
    for start in range(0, WIDTH, 256):
        columns = slice(start, start + 256)
        grad_ref[:, columns] = jnp.dot(
            context_ref[...], c_ref[:, columns], preferred_element_type=F32
        ).astype(BF16)


def project_kernel(
    place_ref, order_ref, from_ref, blocks_ref, keep_ref, send_ref, context_ref, held_ref, weight_ref, sems, sem, out_sems
):
    copies = [pltpu.make_async_copy(from_ref, context_ref, sem)]
    copies[0].start()
    for slot in range(4):
        source = blocks_ref.at[order_ref[16 * place_ref[2] + 12 + slot]]
        copies.append(pltpu.make_async_copy(source, weight_ref.at[slot * HEAD : (slot + 1) * HEAD], sems.at[slot]))
        copies[-1].start()
    for copy in copies:
        copy.wait()
    stores = []
    for part in (1, 3, 0, 2):
        projected = lax.dot_general(
            context_ref[:, part * ROWS : (part + 1) * ROWS],
            weight_ref[...],
            (((0,), (0,)), ((), ())),
            preferred_element_type=F32,
        )
        held_ref[part] = projected.astype(BF16)
        target = send_ref if part % 2 else keep_ref
        stores.append(pltpu.make_async_copy(held_ref.at[part], target.at[part // 2], out_sems.at[part]))
        stores[-1].start()
    for store in stores:
        store.wait()


def sum_kernel(terms_ref, copies_ref):
    total = terms_ref[0].astype(F32)
    for i in range(1, terms_ref.shape[0]):
        total = total + terms_ref[i].astype(F32)
    total = total.astype(BF16)
    for i in range(copies_ref.shape[0]):
        copies_ref[i] = total


VMEM = pl.BlockSpec(memory_space=pltpu.VMEM)
SMEM = pl.BlockSpec(memory_space=pltpu.SMEM)
HBM = pl.BlockSpec(memory_space=pltpu.HBM)
DMA = pltpu.SemaphoreType.DMA


def call(kernel, out_shape, in_specs, out_specs, scratch=(), limit=60 << 20, flops=0, read=0):
    return pl.pallas_call(
        kernel,
        out_shape=out_shape,
        in_specs=in_specs,
        out_specs=out_specs,
        scratch_shapes=scratch,
        compiler_params=pltpu.CompilerParams(vmem_limit_bytes=limit),
        cost_estimate=pl.CostEstimate(flops=flops, bytes_accessed=read, transcendentals=0),
    )


def array(*shape):
    return jax.ShapeDtypeStruct(shape, BF16)


def sum_of(terms, copies):
    return call(
        sum_kernel,
        array(copies, *terms.shape[1:]),
        [VMEM],
        VMEM,
        limit=16 << 20,
        read=2 * (copies + terms.shape[0]) * 40 * WIDTH
    )(terms)


def shards(patches, ln_gain, qkv_weight, proj_weight, out_cotangent, tile_counts, segment_ids):
    core = lax.axis_index("core")
    half = lax.axis_index("z_pair")
    x = lax.axis_index("x")
    shard = lax.axis_index("y_lo") * 4 + x
    place = jnp.stack([2 * shard + half, core, half])
    sends, orders = jnp.asarray(SENDS), jnp.asarray(ORDERS)

    def to_core(value):
        return lax.ppermute(value, "core", CORE_SWAP)

    def to_pair(value):
        return lax.ppermute(value, "z_pair", PAIR_SWAP)

    message, own = call(
        front_kernel,
        (array(ROWS + NOTE, WIDTH), array(8, 2, HEAD, WIDTH)),
        [SMEM, SMEM, SMEM, HBM, VMEM, VMEM, HBM, HBM],
        (HBM, HBM),
        [
            pltpu.VMEM((ROWS, WIDTH), BF16),
            pltpu.VMEM((ROWS + NOTE, WIDTH), BF16),
            pltpu.VMEM((2, HEAD, WIDTH), BF16),
            DMA((2,)),
            DMA((16,)),
            DMA((2,)),
        ],
        read=6 << 20,
    )(
        place,
        sends,
        tile_counts,
        patches,
        ln_gain,
        segment_ids,
        qkv_weight.T.reshape(6, HEAD, WIDTH),
        proj_weight.reshape(2, HEAD, WIDTH),
    )
    blocks = lax.all_to_all(own, FSDP, 0, 0).reshape(16, HEAD, WIDTH)

    message_pair = to_pair(message)
    message_core = to_core(message)
    cotangent_core = to_core(out_cotangent)
    message_pair, cotangent_late = lax.optimization_barrier((message_pair, out_cotangent))
    message_both = to_core(message_pair)
    cotangent_pair = to_pair(cotangent_late)

    context = call(
        attention_kernel,
        array(4 * HEAD, 4 * ROWS),
        [SMEM, SMEM] + [HBM] * 5,
        HBM,
        [
            pltpu.VMEM((4, ROWS + NOTE, WIDTH), BF16),
            pltpu.VMEM((12 * HEAD, WIDTH), BF16),
            pltpu.VMEM((4 * HEAD, 4 * ROWS), BF16),
            DMA((4,)),
            DMA((12,)),
            DMA,
        ],
        limit=52 << 20,
        flops=2 * 1024 * 1280 * 960 + 4 * 16 * 256 * 256 * 128,
        read=8 << 20,
    )(place, orders, message, message_core, message_pair, message_both, blocks)

    context, cotangent_pair = lax.optimization_barrier((context, cotangent_pair))
    cotangent_both = to_core(cotangent_pair)

    grad = call(
        gradient_kernel,
        array(4 * HEAD, WIDTH),
        [HBM] * 5,
        VMEM,
        [pltpu.VMEM((4 * HEAD, 4 * ROWS), BF16), pltpu.VMEM((4 * ROWS, WIDTH), BF16), DMA((5,))],
        flops=2 * 1024 * 1280 * 320,
        read=4 << 20,
    )(context, out_cotangent, cotangent_core, cotangent_pair, cotangent_both)

    keep_out, send_out = call(
        project_kernel,
        (array(2, ROWS, WIDTH), array(2, ROWS, WIDTH)),
        [SMEM, SMEM, HBM, HBM],
        (HBM, HBM),
        [
            pltpu.VMEM((4 * HEAD, 4 * ROWS), BF16),
            pltpu.VMEM((4, ROWS, WIDTH), BF16),
            pltpu.VMEM((4 * HEAD, WIDTH), BF16),
            DMA((4,)),
            DMA,
            DMA((4,)),
        ],
        limit=52 << 20,
        flops=2 * 1024 * 1280 * 320,
        read=6 << 20,
    )(place, orders, context, blocks)

    from_core = to_core(send_out)
    for_pair = (keep_out[1].astype(F32) + from_core[1].astype(F32)).astype(BF16)
    grad = lax.all_to_all(grad.reshape(8, 40, WIDTH), FSDP, 0, 0)
    grad, for_pair = lax.optimization_barrier((grad, for_pair))
    from_pair = to_pair(for_pair)
    grad = sum_of(grad, Y_HI)
    grad = lax.all_to_all(grad, "y_hi", 0, 0)
    grad, from_pair = lax.optimization_barrier((grad, from_pair))
    grad = sum_of(grad, Z_QUAD)

    projected = keep_out[0].astype(F32) + from_core[0].astype(F32) + from_pair.astype(F32)
    alive = lax.iota(jnp.int32, ROWS) < tile_counts[0] * TILE
    output = jnp.where(alive[:, None], patches.astype(F32) + projected, F32(0.0)).astype(BF16)

    grad = lax.all_to_all(grad, "z_quad", 0, 0)
    grad, output = lax.optimization_barrier((grad, output))
    grad = sum_of(grad, 1)[0]

    first = lax.ppermute(grad, ("x", "z_pair"), TO_OWNER)
    second = lax.ppermute(grad, ("x", "z_pair"), ACROSS)
    owner = ((x == 0) | (x == 3)) == (half == 1)
    near = jnp.where(owner, grad, first)
    far = jnp.where(owner, first, second)
    even = x % 2 == 0
    head_grad = jnp.concatenate([jnp.where(even, near, far), jnp.where(even, far, near)])
    other_grad = to_core(head_grad)
    proj_grad = jnp.concatenate(
        [jnp.where(core == 0, head_grad, other_grad), jnp.where(core == 0, other_grad, head_grad)]
    )
    return output, proj_grad


def solution(mesh):
    fine = Mesh(mesh.devices.reshape(2, 4, Y_HI, Z_QUAD, Z_PAIR, CORES), AXES)
    return jax.shard_map(
        shards,
        mesh=fine,
        in_specs=(P(AXES, None), P(), P(None, FSDP), P(FSDP, None), P(AXES, None), P(AXES), P(AXES)),
        out_specs=(P(AXES, None), P(FSDP, None)),
        check_vma=False,
    )
```

```python
import math

import jax
import jax.numpy as jnp
import numpy as np
from jax import lax
from jax.experimental import pallas as pl
from jax.experimental.pallas import tpu as pltpu
from jax.sharding import Mesh
from jax.sharding import PartitionSpec as P

HEADS = 16
HEAD = 80
TILE = 128
ROWS = 256
NOTE = 16
WIDTH = 1280
EPSILON = 1e-06
BF16 = jnp.bfloat16
F32 = jnp.float32

Y_HI, Z_QUAD, Z_PAIR, CORES = 4, 4, 2, 2
AXES = ("y_lo", "x", "y_hi", "z_quad", "z_pair", "core")
FSDP = ("y_lo", "x")

HEAD_SETS = ((1, 2, 5, 6), (0, 3, 4, 7))


def block_tables():
    sends = np.zeros((8, 2, 2), np.int32)
    orders = np.zeros((2, 16), np.int32)
    for half, heads in enumerate(HEAD_SETS):
        for shard in range(8):
            picked = [k for k in range(3) if (3 * shard + k) % 8 in heads] + ([3] if shard in heads else [])
            assert len(picked) == 2
            for place, k in enumerate(picked):
                sends[shard, half, place] = k
                if k == 3:
                    slot = 12 + heads.index(shard)
                else:
                    kind, m = divmod(3 * shard + k, 8)
                    slot = 4 * kind + heads.index(m)
                orders[half, slot] = 2 * shard + place
    return sends.reshape(-1), orders.reshape(-1)


SENDS, ORDERS = block_tables()


def owns(x, half):
    return int(x in (0, 3)) == half


CORE_SWAP = [(0, 1), (1, 0)]
PAIR_SWAP = [(0, 1), (1, 0)]
TO_OWNER = [
    (2 * x + half, 2 * x + (1 - half) if owns(x, half) else 2 * (x ^ 1) + half) for x in range(4) for half in range(2)
]
ACROSS = [(2 * x + half, 2 * (x ^ 1) + (1 - half)) for x in range(4) for half in range(2) if not owns(x, half)]


def front_kernel(
    place_ref,
    sends_ref,
    count_ref,
    patches_ref,
    gain_ref,
    images_ref,
    qkv_ref,
    proj_ref,
    out_ref,
    blocks_ref,
    rows_ref,
    message_ref,
    held_ref,
    read_sems,
    write_sems,
    sems,
):
    fetch = pltpu.make_async_copy(patches_ref, rows_ref, sems.at[0])
    fetch.start()
    core = place_ref[1]
    for i in range(2):
        choice = sends_ref[2 * place_ref[0] + i]

        @pl.when(choice < 3)
        def _():
            pltpu.make_async_copy(qkv_ref.at[2 * jnp.minimum(choice, 2) + core], held_ref.at[i], read_sems.at[i]).start()

        @pl.when(choice == 3)
        def _():
            pltpu.make_async_copy(proj_ref.at[core], held_ref.at[i], read_sems.at[i]).start()

    copies = []
    for i in range(2):
        pltpu.make_async_copy(proj_ref.at[0], held_ref.at[i], read_sems.at[i]).wait()
        for peer in range(8):
            copies.append(pltpu.make_async_copy(held_ref.at[i], blocks_ref.at[peer, i], write_sems.at[8 * i + peer]))
            copies[-1].start()

    fetch.wait()
    inputs = rows_ref[...].astype(F32)
    row_mean = jnp.mean(inputs, axis=1, keepdims=True)
    centred = inputs - row_mean
    variance = jnp.mean(centred * centred, axis=1, keepdims=True)
    message_ref[:ROWS, :] = (centred * lax.rsqrt(variance + EPSILON) * gain_ref[...].reshape(1, WIDTH)).astype(BF16)
    dead = lax.broadcasted_iota(jnp.int32, (1, ROWS), 1) >= count_ref[0] * TILE
    code = (images_ref[...].reshape(1, ROWS) + jnp.where(dead, 64, 0)).astype(F32)
    message_ref[ROWS:, :] = jnp.zeros((NOTE, WIDTH), BF16)
    message_ref[ROWS:, :ROWS] = jnp.broadcast_to(code, (NOTE, ROWS)).astype(BF16)
    copies.append(pltpu.make_async_copy(message_ref, out_ref, sems.at[1]))
    copies[-1].start()
    for copy in copies:
        copy.wait()


def attention_kernel(
    place_ref,
    order_ref,
    x0_ref,
    x1_ref,
    x2_ref,
    x3_ref,
    blocks_ref,
    c0_ref,
    c1_ref,
    c2_ref,
    c3_ref,
    out_ref,
    grad_ref,
    x_ref,
    weight_ref,
    context_ref,
    c_ref,
    x_sems,
    sems,
    c_sems,
    out_sem,
):
    scale = HEAD**-0.5 * math.log2(math.e)
    hidden = -1e30 * HEAD**0.5
    copies = []
    for slot in range(12):
        source = blocks_ref.at[order_ref[16 * place_ref[2] + slot]]
        copies.append(pltpu.make_async_copy(source, weight_ref.at[slot * HEAD : (slot + 1) * HEAD], sems.at[slot]))
    arrivals = [
        pltpu.make_async_copy(ref, x_ref.at[part], x_sems.at[part])
        for part, ref in enumerate((x0_ref, x1_ref, x2_ref, x3_ref))
    ]
    cotangents = [
        pltpu.make_async_copy(ref, c_ref.at[part * ROWS : (part + 1) * ROWS], c_sems.at[part])
        for part, ref in enumerate((c0_ref, c1_ref, c2_ref, c3_ref))
    ]
    for copy in copies + arrivals + cotangents:
        copy.start()
    for copy in copies + arrivals:
        copy.wait()
    for part in range(4):
        mixed = lax.dot_general(
            weight_ref[...], x_ref[part, :ROWS, :], (((1,), (1,)), ((), ())), preferred_element_type=F32
        ).astype(BF16)
        code = x_ref[part, ROWS:, :ROWS].astype(F32)[0:1, :]
        square = jnp.broadcast_to(code, (ROWS, ROWS))
        allowed = square == square.T
        alive = code < 64.0
        for head in range(4):
            queries = mixed[head * HEAD : (head + 1) * HEAD, :]
            keyset = mixed[(4 + head) * HEAD : (5 + head) * HEAD, :]
            valueset = mixed[(8 + head) * HEAD : (9 + head) * HEAD, :]
            scores = lax.dot_general(keyset, queries, (((0,), (0,)), ((), ())), preferred_element_type=F32)
            scores = jnp.where(allowed, scores, hidden)
            peak = jnp.max(scores, axis=0, keepdims=True)
            weights = jnp.exp2((scores - peak) * scale)
            total = jnp.sum(weights, axis=0, keepdims=True)
            context = jnp.dot(valueset, weights.astype(BF16), preferred_element_type=F32)
            context = jnp.where(alive, context / total, 0.0)
            context_ref[head * HEAD : (head + 1) * HEAD, part * ROWS : (part + 1) * ROWS] = context.astype(BF16)
    store = pltpu.make_async_copy(context_ref, out_ref, out_sem)
    store.start()
    for copy in cotangents:
        copy.wait()
    for start in range(0, WIDTH, 256):
        columns = slice(start, start + 256)
        grad_ref[:, columns] = jnp.dot(
            context_ref[...], c_ref[:, columns], preferred_element_type=F32
        ).astype(BF16)
    store.wait()


def project_kernel(
    place_ref, order_ref, from_ref, blocks_ref, keep_ref, send_ref, context_ref, held_ref, weight_ref, sems, sem, out_sems
):
    copies = [pltpu.make_async_copy(from_ref, context_ref, sem)]
    copies[0].start()
    for slot in range(4):
        source = blocks_ref.at[order_ref[16 * place_ref[2] + 12 + slot]]
        copies.append(pltpu.make_async_copy(source, weight_ref.at[slot * HEAD : (slot + 1) * HEAD], sems.at[slot]))
        copies[-1].start()
    for copy in copies:
        copy.wait()
    stores = []
    for part in (1, 3, 0, 2):
        projected = lax.dot_general(
            context_ref[:, part * ROWS : (part + 1) * ROWS],
            weight_ref[...],
            (((0,), (0,)), ((), ())),
            preferred_element_type=F32,
        )
        held_ref[part] = projected.astype(BF16)
        target = send_ref if part % 2 else keep_ref
        stores.append(pltpu.make_async_copy(held_ref.at[part], target.at[part // 2], out_sems.at[part]))
        stores[-1].start()
    for store in stores:
        store.wait()


def sum_kernel(terms_ref, copies_ref):
    total = terms_ref[0].astype(F32)
    for i in range(1, terms_ref.shape[0]):
        total = total + terms_ref[i].astype(F32)
    total = total.astype(BF16)
    for i in range(copies_ref.shape[0]):
        copies_ref[i] = total


VMEM = pl.BlockSpec(memory_space=pltpu.VMEM)
SMEM = pl.BlockSpec(memory_space=pltpu.SMEM)
HBM = pl.BlockSpec(memory_space=pltpu.HBM)
DMA = pltpu.SemaphoreType.DMA


def call(kernel, out_shape, in_specs, out_specs, scratch=(), limit=60 << 20, flops=0, read=0):
    return pl.pallas_call(
        kernel,
        out_shape=out_shape,
        in_specs=in_specs,
        out_specs=out_specs,
        scratch_shapes=scratch,
        compiler_params=pltpu.CompilerParams(vmem_limit_bytes=limit),
        cost_estimate=pl.CostEstimate(flops=flops, bytes_accessed=read, transcendentals=0),
    )


def array(*shape):
    return jax.ShapeDtypeStruct(shape, BF16)


def sum_of(terms, copies):
    return call(
        sum_kernel,
        array(copies, *terms.shape[1:]),
        [VMEM],
        VMEM,
        limit=16 << 20,
        read=2 * (copies + terms.shape[0]) * 40 * WIDTH
    )(terms)


def shards(patches, ln_gain, qkv_weight, proj_weight, out_cotangent, tile_counts, segment_ids):
    core = lax.axis_index("core")
    half = lax.axis_index("z_pair")
    x = lax.axis_index("x")
    shard = lax.axis_index("y_lo") * 4 + x
    place = jnp.stack([2 * shard + half, core, half])
    sends, orders = jnp.asarray(SENDS), jnp.asarray(ORDERS)

    def to_core(value):
        return lax.ppermute(value, "core", CORE_SWAP)

    def to_pair(value):
        return lax.ppermute(value, "z_pair", PAIR_SWAP)

    message, own = call(
        front_kernel,
        (array(ROWS + NOTE, WIDTH), array(8, 2, HEAD, WIDTH)),
        [SMEM, SMEM, SMEM, HBM, VMEM, VMEM, HBM, HBM],
        (HBM, HBM),
        [
            pltpu.VMEM((ROWS, WIDTH), BF16),
            pltpu.VMEM((ROWS + NOTE, WIDTH), BF16),
            pltpu.VMEM((2, HEAD, WIDTH), BF16),
            DMA((2,)),
            DMA((16,)),
            DMA((2,)),
        ],
        read=6 << 20,
    )(
        place,
        sends,
        tile_counts,
        patches,
        ln_gain,
        segment_ids,
        qkv_weight.T.reshape(6, HEAD, WIDTH),
        proj_weight.reshape(2, HEAD, WIDTH),
    )
    blocks = lax.all_to_all(own, FSDP, 0, 0).reshape(16, HEAD, WIDTH)

    message_pair = to_pair(message)
    cotangent_pair = to_pair(out_cotangent)
    message_core = to_core(message)
    cotangent_core = to_core(out_cotangent)
    message_both = to_core(message_pair)
    cotangent_both = to_core(cotangent_pair)

    context, grad = call(
        attention_kernel,
        (array(4 * HEAD, 4 * ROWS), array(4 * HEAD, WIDTH)),
        [SMEM, SMEM] + [HBM] * 9,
        (HBM, VMEM),
        [
            pltpu.VMEM((4, ROWS + NOTE, WIDTH), BF16),
            pltpu.VMEM((12 * HEAD, WIDTH), BF16),
            pltpu.VMEM((4 * HEAD, 4 * ROWS), BF16),
            pltpu.VMEM((4 * ROWS, WIDTH), BF16),
            DMA((4,)),
            DMA((12,)),
            DMA((4,)),
            DMA,
        ],
        limit=52 << 20,
        flops=2 * 1024 * 1280 * 1280 + 4 * 16 * 256 * 256 * 128,
        read=12 << 20,
    )(
        place,
        orders,
        message,
        message_core,
        message_pair,
        message_both,
        blocks,
        out_cotangent,
        cotangent_core,
        cotangent_pair,
        cotangent_both,
    )

    keep_out, send_out = call(
        project_kernel,
        (array(2, ROWS, WIDTH), array(2, ROWS, WIDTH)),
        [SMEM, SMEM, HBM, HBM],
        (HBM, HBM),
        [
            pltpu.VMEM((4 * HEAD, 4 * ROWS), BF16),
            pltpu.VMEM((4, ROWS, WIDTH), BF16),
            pltpu.VMEM((4 * HEAD, WIDTH), BF16),
            DMA((4,)),
            DMA,
            DMA((4,)),
        ],
        limit=52 << 20,
        flops=2 * 1024 * 1280 * 320,
        read=6 << 20,
    )(place, orders, context, blocks)

    grad = lax.all_to_all(grad.reshape(8, 40, WIDTH), FSDP, 0, 0)
    grad, keep_late = lax.optimization_barrier((grad, keep_out))
    grad = sum_of(grad, Z_QUAD)
    from_core = to_core(send_out)
    for_pair = (keep_out[1].astype(F32) + from_core[1].astype(F32)).astype(BF16)
    grad = lax.all_to_all(grad, "z_quad", 0, 0)
    grad, from_core_late = lax.optimization_barrier((grad, from_core))
    grad = sum_of(grad, Y_HI)
    from_pair = to_pair(for_pair)
    projected = keep_late[0].astype(F32) + from_core_late[0].astype(F32) + from_pair.astype(F32)
    alive = lax.iota(jnp.int32, ROWS) < tile_counts[0] * TILE
    output = jnp.where(alive[:, None], patches.astype(F32) + projected, F32(0.0)).astype(BF16)
    grad = lax.all_to_all(grad, "y_hi", 0, 0)
    grad, output = lax.optimization_barrier((grad, output))
    grad = sum_of(grad, 1)[0]

    first = lax.ppermute(grad, ("x", "z_pair"), TO_OWNER)
    second = lax.ppermute(grad, ("x", "z_pair"), ACROSS)
    owner = ((x == 0) | (x == 3)) == (half == 1)
    two = lax.broadcasted_iota(jnp.int32, (2, 1, 1), 0)
    head_grad = jnp.where(two == x % 2, jnp.where(owner, grad, first), jnp.where(owner, first, second))
    head_grad = head_grad.reshape(HEAD, WIDTH)
    proj_grad = jnp.where(two == core, head_grad, to_core(head_grad)).reshape(2 * HEAD, WIDTH)
    return output, proj_grad


def solution(mesh):
    fine = Mesh(mesh.devices.reshape(2, 4, Y_HI, Z_QUAD, Z_PAIR, CORES), AXES)
    return jax.shard_map(
        shards,
        mesh=fine,
        in_specs=(P(AXES, None), P(), P(None, FSDP), P(FSDP, None), P(AXES, None), P(AXES), P(AXES)),
        out_specs=(P(AXES, None), P(FSDP, None)),
        check_vma=False,
    )
```

```python
import math

import jax
import jax.numpy as jnp
import numpy as np
from jax import lax
from jax.experimental import pallas as pl
from jax.experimental.pallas import tpu as pltpu
from jax.sharding import Mesh
from jax.sharding import PartitionSpec as P

HEADS = 16
HEAD = 80
TILE = 128
ROWS = 256
NOTE = 16
WIDTH = 1280
EPSILON = 1e-06
BF16 = jnp.bfloat16
F32 = jnp.float32

Y_HI, Z_QUAD, Z_PAIR, CORES = 4, 4, 2, 2
AXES = ("y_lo", "x", "y_hi", "z_quad", "z_pair", "core")
FSDP = ("y_lo", "x")

HEAD_SETS = ((1, 2, 5, 6), (0, 3, 4, 7))


def block_tables():
    sends = np.zeros((8, 2, 2), np.int32)
    orders = np.zeros((2, 16), np.int32)
    for half, heads in enumerate(HEAD_SETS):
        for shard in range(8):
            picked = [k for k in range(3) if (3 * shard + k) % 8 in heads] + ([3] if shard in heads else [])
            assert len(picked) == 2
            for place, k in enumerate(picked):
                sends[shard, half, place] = k
                if k == 3:
                    slot = 12 + heads.index(shard)
                else:
                    kind, m = divmod(3 * shard + k, 8)
                    slot = 4 * kind + heads.index(m)
                orders[half, slot] = 2 * shard + place
    return sends.reshape(-1), orders.reshape(-1)


SENDS, ORDERS = block_tables()


def owns(x, half):
    return int(x in (0, 3)) == half


CORE_SWAP = [(0, 1), (1, 0)]
PAIR_SWAP = [(0, 1), (1, 0)]
TO_OWNER = [
    (2 * x + half, 2 * x + (1 - half) if owns(x, half) else 2 * (x ^ 1) + half) for x in range(4) for half in range(2)
]
ACROSS = [(2 * x + half, 2 * (x ^ 1) + (1 - half)) for x in range(4) for half in range(2) if not owns(x, half)]


def half_of(place_ref):
    return place_ref[0] // CORES % Z_PAIR


def front_kernel(
    place_ref,
    sends_ref,
    count_ref,
    patches_ref,
    gain_ref,
    images_ref,
    qkv_ref,
    proj_ref,
    out_ref,
    blocks_ref,
    rows_ref,
    message_ref,
    held_ref,
    read_sems,
    write_sems,
    sems,
):
    shard = place_ref[0] // (Y_HI * Z_QUAD * Z_PAIR * CORES)
    core = place_ref[0] % CORES
    for i in range(2):
        choice = sends_ref[4 * shard + 2 * half_of(place_ref) + i]

        @pl.when(choice < 3)
        def _():
            pltpu.make_async_copy(qkv_ref.at[2 * jnp.minimum(choice, 2) + core], held_ref.at[i], read_sems.at[i]).start()

        @pl.when(choice == 3)
        def _():
            pltpu.make_async_copy(proj_ref.at[core], held_ref.at[i], read_sems.at[i]).start()

    fetch = pltpu.make_async_copy(patches_ref, rows_ref, sems.at[0])
    fetch.start()
    copies = []
    for i in range(2):
        pltpu.make_async_copy(proj_ref.at[0], held_ref.at[i], read_sems.at[i]).wait()
        for peer in range(8):
            copies.append(pltpu.make_async_copy(held_ref.at[i], blocks_ref.at[peer, i], write_sems.at[8 * i + peer]))
            copies[-1].start()

    fetch.wait()
    inputs = rows_ref[...].astype(F32)
    row_mean = jnp.mean(inputs, axis=1, keepdims=True)
    centred = inputs - row_mean
    variance = jnp.mean(centred * centred, axis=1, keepdims=True)
    message_ref[:ROWS, :] = (centred * lax.rsqrt(variance + EPSILON) * gain_ref[...].reshape(1, WIDTH)).astype(BF16)
    dead = lax.broadcasted_iota(jnp.int32, (1, ROWS), 1) >= count_ref[0] * TILE
    code = (images_ref[...].reshape(1, ROWS) + jnp.where(dead, 64, 0)).astype(F32)
    message_ref[ROWS:, :] = jnp.zeros((NOTE, WIDTH), BF16)
    message_ref[ROWS:, :ROWS] = jnp.broadcast_to(code, (NOTE, ROWS)).astype(BF16)
    copies.append(pltpu.make_async_copy(message_ref, out_ref, sems.at[1]))
    copies[-1].start()
    for copy in copies:
        copy.wait()


def attention_kernel(
    place_ref,
    order_ref,
    x0_ref,
    x1_ref,
    x2_ref,
    x3_ref,
    blocks_ref,
    c0_ref,
    c1_ref,
    c2_ref,
    c3_ref,
    out_ref,
    grad_ref,
    x_ref,
    weight_ref,
    context_ref,
    c_ref,
    x_sems,
    sems,
    c_sems,
    out_sem,
):
    scale = HEAD**-0.5 * math.log2(math.e)
    hidden = -1e30 * HEAD**0.5
    copies = []
    for slot in range(12):
        source = blocks_ref.at[order_ref[16 * half_of(place_ref) + slot]]
        copies.append(pltpu.make_async_copy(source, weight_ref.at[slot * HEAD : (slot + 1) * HEAD], sems.at[slot]))
    arrivals = [
        pltpu.make_async_copy(ref, x_ref.at[part], x_sems.at[part])
        for part, ref in enumerate((x0_ref, x1_ref, x2_ref, x3_ref))
    ]
    cotangents = [
        pltpu.make_async_copy(ref, c_ref.at[part * ROWS : (part + 1) * ROWS], c_sems.at[part])
        for part, ref in enumerate((c0_ref, c1_ref, c2_ref, c3_ref))
    ]
    for copy in copies + arrivals + cotangents:
        copy.start()
    for copy in copies + arrivals:
        copy.wait()
    everything = [
        lax.dot_general(
            weight_ref[...], x_ref[part, :ROWS, :], (((1,), (1,)), ((), ())), preferred_element_type=F32
        ).astype(BF16)
        for part in range(4)
    ]
    for part in range(4):
        mixed = everything[part]
        code = x_ref[part, ROWS:, :ROWS].astype(F32)[0:1, :]
        square = jnp.broadcast_to(code, (ROWS, ROWS))
        allowed = square == square.T
        alive = code < 64.0
        def piece(kind, head):
            return mixed[(4 * kind + head) * HEAD : (4 * kind + head + 1) * HEAD, :]

        scores = [
            lax.dot_general(piece(1, head), piece(0, head), (((0,), (0,)), ((), ())), preferred_element_type=F32)
            for head in range(4)
        ]
        weights, totals = [], []
        for head in range(4):
            masked = jnp.where(allowed, scores[head], hidden)
            peak = jnp.max(masked, axis=0, keepdims=True)
            weight = jnp.exp2((masked - peak) * scale)
            totals.append(jnp.sum(weight, axis=0, keepdims=True))
            weights.append(weight.astype(BF16))
        for head in range(4):
            context = jnp.dot(piece(2, head), weights[head], preferred_element_type=F32)
            context = jnp.where(alive, context / totals[head], 0.0)
            context_ref[head * HEAD : (head + 1) * HEAD, part * ROWS : (part + 1) * ROWS] = context.astype(BF16)
    store = pltpu.make_async_copy(context_ref, out_ref, out_sem)
    store.start()
    for copy in cotangents:
        copy.wait()
    for start in range(0, WIDTH, 256):
        columns = slice(start, start + 256)
        grad_ref[:, columns] = jnp.dot(
            context_ref[...], c_ref[:, columns], preferred_element_type=F32
        ).astype(BF16)
    store.wait()


def project_kernel(
    place_ref, order_ref, from_ref, blocks_ref, keep_ref, send_ref, context_ref, held_ref, weight_ref, sems, sem, out_sems
):
    copies = [pltpu.make_async_copy(from_ref, context_ref, sem)]
    copies[0].start()
    for slot in range(4):
        source = blocks_ref.at[order_ref[16 * half_of(place_ref) + 12 + slot]]
        copies.append(pltpu.make_async_copy(source, weight_ref.at[slot * HEAD : (slot + 1) * HEAD], sems.at[slot]))
        copies[-1].start()
    for copy in copies:
        copy.wait()
    stores = []
    for part in (1, 3, 0, 2):
        projected = lax.dot_general(
            context_ref[:, part * ROWS : (part + 1) * ROWS],
            weight_ref[...],
            (((0,), (0,)), ((), ())),
            preferred_element_type=F32,
        )
        held_ref[part] = projected.astype(BF16)
        target = send_ref if part % 2 else keep_ref
        stores.append(pltpu.make_async_copy(held_ref.at[part], target.at[part // 2], out_sems.at[part]))
        stores[-1].start()
    for store in stores:
        store.wait()


def sum_kernel(terms_ref, copies_ref):
    total = terms_ref[0].astype(F32)
    for i in range(1, terms_ref.shape[0]):
        total = total + terms_ref[i].astype(F32)
    total = total.astype(BF16)
    for i in range(copies_ref.shape[0]):
        copies_ref[i] = total


VMEM = pl.BlockSpec(memory_space=pltpu.VMEM)
SMEM = pl.BlockSpec(memory_space=pltpu.SMEM)
HBM = pl.BlockSpec(memory_space=pltpu.HBM)
DMA = pltpu.SemaphoreType.DMA


def call(kernel, out_shape, in_specs, out_specs, scratch=(), limit=60 << 20, flops=0, read=0):
    return pl.pallas_call(
        kernel,
        out_shape=out_shape,
        in_specs=in_specs,
        out_specs=out_specs,
        scratch_shapes=scratch,
        compiler_params=pltpu.CompilerParams(vmem_limit_bytes=limit),
        cost_estimate=pl.CostEstimate(flops=flops, bytes_accessed=read, transcendentals=0),
    )


def array(*shape):
    return jax.ShapeDtypeStruct(shape, BF16)


def sum_of(terms, copies):
    return call(
        sum_kernel,
        array(copies, *terms.shape[1:]),
        [VMEM],
        VMEM,
        limit=16 << 20,
        read=2 * (copies + terms.shape[0]) * 40 * WIDTH
    )(terms)


def shards(patches, ln_gain, qkv_weight, proj_weight, out_cotangent, tile_counts, segment_ids):
    core = lax.axis_index("core")
    half = lax.axis_index("z_pair")
    x = lax.axis_index("x")
    shard = lax.axis_index("y_lo") * 4 + x
    place = lax.axis_index(AXES).reshape(1)
    sends, orders = jnp.asarray(SENDS), jnp.asarray(ORDERS)

    def to_core(value):
        return lax.ppermute(value, "core", CORE_SWAP)

    def to_pair(value):
        return lax.ppermute(value, "z_pair", PAIR_SWAP)

    message, own = call(
        front_kernel,
        (array(ROWS + NOTE, WIDTH), array(8, 2, HEAD, WIDTH)),
        [SMEM, SMEM, SMEM, HBM, VMEM, VMEM, HBM, HBM],
        (HBM, HBM),
        [
            pltpu.VMEM((ROWS, WIDTH), BF16),
            pltpu.VMEM((ROWS + NOTE, WIDTH), BF16),
            pltpu.VMEM((2, HEAD, WIDTH), BF16),
            DMA((2,)),
            DMA((16,)),
            DMA((2,)),
        ],
        read=6 << 20,
    )(
        place,
        sends,
        tile_counts,
        patches,
        ln_gain,
        segment_ids,
        qkv_weight.T.reshape(6, HEAD, WIDTH),
        proj_weight.reshape(2, HEAD, WIDTH),
    )
    blocks = lax.all_to_all(own, FSDP, 0, 0).reshape(16, HEAD, WIDTH)

    message_pair = to_pair(message)
    cotangent_pair = to_pair(out_cotangent)
    message_core = to_core(message)
    cotangent_core = to_core(out_cotangent)
    message_both = to_core(message_pair)
    cotangent_both = to_core(cotangent_pair)

    context, grad = call(
        attention_kernel,
        (array(4 * HEAD, 4 * ROWS), array(4 * HEAD, WIDTH)),
        [SMEM, SMEM] + [HBM] * 9,
        (HBM, VMEM),
        [
            pltpu.VMEM((4, ROWS + NOTE, WIDTH), BF16),
            pltpu.VMEM((12 * HEAD, WIDTH), BF16),
            pltpu.VMEM((4 * HEAD, 4 * ROWS), BF16),
            pltpu.VMEM((4 * ROWS, WIDTH), BF16),
            DMA((4,)),
            DMA((12,)),
            DMA((4,)),
            DMA,
        ],
        limit=52 << 20,
        flops=2 * 1024 * 1280 * 1280 + 4 * 16 * 256 * 256 * 128,
        read=12 << 20,
    )(
        place,
        orders,
        message,
        message_core,
        message_pair,
        message_both,
        blocks,
        out_cotangent,
        cotangent_core,
        cotangent_pair,
        cotangent_both,
    )

    keep_out, send_out = call(
        project_kernel,
        (array(2, ROWS, WIDTH), array(2, ROWS, WIDTH)),
        [SMEM, SMEM, HBM, HBM],
        (HBM, HBM),
        [
            pltpu.VMEM((4 * HEAD, 4 * ROWS), BF16),
            pltpu.VMEM((4, ROWS, WIDTH), BF16),
            pltpu.VMEM((4 * HEAD, WIDTH), BF16),
            DMA((4,)),
            DMA,
            DMA((4,)),
        ],
        limit=52 << 20,
        flops=2 * 1024 * 1280 * 320,
        read=6 << 20,
    )(place, orders, context, blocks)

    grad = lax.all_to_all(grad.reshape(8, 40, WIDTH), FSDP, 0, 0)
    grad, keep_late = lax.optimization_barrier((grad, keep_out))
    grad = sum_of(grad, Z_QUAD)
    from_core = to_core(send_out)
    for_pair = (keep_out[1].astype(F32) + from_core[1].astype(F32)).astype(BF16)
    grad = lax.all_to_all(grad, "z_quad", 0, 0)
    grad, from_core_late = lax.optimization_barrier((grad, from_core))
    grad = sum_of(grad, Y_HI)
    from_pair = to_pair(for_pair)
    grad = lax.all_to_all(grad, "y_hi", 0, 0)
    grad, from_pair = lax.optimization_barrier((grad, from_pair))
    grad = sum_of(grad, 1)[0]

    first = lax.ppermute(grad, ("x", "z_pair"), TO_OWNER)
    second = lax.ppermute(grad, ("x", "z_pair"), ACROSS)
    projected = keep_late[0].astype(F32) + from_core_late[0].astype(F32) + from_pair.astype(F32)
    alive = lax.iota(jnp.int32, ROWS) < tile_counts[0] * TILE
    output = jnp.where(alive[:, None], patches.astype(F32) + projected, F32(0.0)).astype(BF16)
    second, output = lax.optimization_barrier((second, output))
    owner = ((x == 0) | (x == 3)) == (half == 1)
    two = lax.broadcasted_iota(jnp.int32, (2, 1, 1), 0)
    head_grad = jnp.where(two == x % 2, jnp.where(owner, grad, first), jnp.where(owner, first, second))
    head_grad = head_grad.reshape(HEAD, WIDTH)
    proj_grad = jnp.where(two == core, head_grad, to_core(head_grad)).reshape(2 * HEAD, WIDTH)
    return output, proj_grad


def solution(mesh):
    fine = Mesh(mesh.devices.reshape(2, 4, Y_HI, Z_QUAD, Z_PAIR, CORES), AXES)
    return jax.shard_map(
        shards,
        mesh=fine,
        in_specs=(P(AXES, None), P(), P(None, FSDP), P(FSDP, None), P(AXES, None), P(AXES), P(AXES)),
        out_specs=(P(AXES, None), P(FSDP, None)),
        check_vma=False,
    )
```

```python
import math

import jax
import jax.numpy as jnp
import numpy as np
from jax import lax
from jax.experimental import pallas as pl
from jax.experimental.pallas import tpu as pltpu
from jax.sharding import Mesh
from jax.sharding import PartitionSpec as P

HEADS = 16
HEAD = 80
TILE = 128
ROWS = 256
NOTE = 16
WIDTH = 1280
EPSILON = 1e-06
BF16 = jnp.bfloat16
F32 = jnp.float32

Y_HI, Z_QUAD, Z_PAIR, CORES = 4, 4, 2, 2
AXES = ("y_lo", "x", "y_hi", "z_quad", "z_pair", "core")
FSDP = ("y_lo", "x")

HEAD_SETS = ((1, 2, 5, 6), (0, 3, 4, 7))


def block_tables():
    sends = np.zeros((8, 2, 2), np.int32)
    orders = np.zeros((2, 16), np.int32)
    for half, heads in enumerate(HEAD_SETS):
        for shard in range(8):
            picked = [k for k in range(3) if (3 * shard + k) % 8 in heads] + ([3] if shard in heads else [])
            assert len(picked) == 2
            for place, k in enumerate(picked):
                sends[shard, half, place] = k
                if k == 3:
                    slot = 12 + heads.index(shard)
                else:
                    kind, m = divmod(3 * shard + k, 8)
                    slot = 4 * kind + heads.index(m)
                orders[half, slot] = 2 * shard + place
    return sends.reshape(-1), orders.reshape(-1)


SENDS, ORDERS = block_tables()


def owns(x, half):
    return int(x in (0, 3)) == half


CORE_SWAP = [(0, 1), (1, 0)]
PAIR_SWAP = [(0, 1), (1, 0)]
TO_OWNER = [
    (2 * x + half, 2 * x + (1 - half) if owns(x, half) else 2 * (x ^ 1) + half) for x in range(4) for half in range(2)
]
ACROSS = [(2 * x + half, 2 * (x ^ 1) + (1 - half)) for x in range(4) for half in range(2) if not owns(x, half)]


def cross_groups(first):
    def place(y, z, core):
        return (y * Z_QUAD + z) * CORES + core

    along_z = [[place(y, z, first) for z in range(Z_QUAD)] for y in range(Y_HI)]
    return along_z + [[place(y, z, 1 - first) for y in range(Y_HI)] for z in range(Z_QUAD)]


def half_of(place_ref):
    return place_ref[0] // CORES % Z_PAIR


def front_kernel(
    place_ref,
    sends_ref,
    count_ref,
    patches_ref,
    gain_ref,
    images_ref,
    qkv_ref,
    proj_ref,
    out_ref,
    blocks_ref,
    rows_ref,
    message_ref,
    held_ref,
    read_sems,
    write_sems,
    sems,
):
    shard = place_ref[0] // (Y_HI * Z_QUAD * Z_PAIR * CORES)
    core = place_ref[0] % CORES
    for i in range(2):
        choice = sends_ref[4 * shard + 2 * half_of(place_ref) + i]

        @pl.when(choice < 3)
        def _():
            pltpu.make_async_copy(qkv_ref.at[2 * jnp.minimum(choice, 2) + core], held_ref.at[i], read_sems.at[i]).start()

        @pl.when(choice == 3)
        def _():
            pltpu.make_async_copy(proj_ref.at[core], held_ref.at[i], read_sems.at[i]).start()

    fetch = pltpu.make_async_copy(patches_ref, rows_ref, sems.at[0])
    fetch.start()
    copies = []
    for i in range(2):
        pltpu.make_async_copy(proj_ref.at[0], held_ref.at[i], read_sems.at[i]).wait()
        for peer in range(8):
            copies.append(pltpu.make_async_copy(held_ref.at[i], blocks_ref.at[peer, i], write_sems.at[8 * i + peer]))
            copies[-1].start()

    fetch.wait()
    inputs = rows_ref[...].astype(F32)
    row_mean = jnp.mean(inputs, axis=1, keepdims=True)
    centred = inputs - row_mean
    variance = jnp.mean(centred * centred, axis=1, keepdims=True)
    message_ref[:ROWS, :] = (centred * lax.rsqrt(variance + EPSILON) * gain_ref[...].reshape(1, WIDTH)).astype(BF16)
    dead = lax.broadcasted_iota(jnp.int32, (1, ROWS), 1) >= count_ref[0] * TILE
    code = (images_ref[...].reshape(1, ROWS) + jnp.where(dead, 64, 0)).astype(F32)
    message_ref[ROWS:, :] = jnp.zeros((NOTE, WIDTH), BF16)
    message_ref[ROWS:, :ROWS] = jnp.broadcast_to(code, (NOTE, ROWS)).astype(BF16)
    copies.append(pltpu.make_async_copy(message_ref, out_ref, sems.at[1]))
    copies[-1].start()
    for copy in copies:
        copy.wait()


def attention_kernel(
    place_ref,
    order_ref,
    x0_ref,
    x1_ref,
    x2_ref,
    x3_ref,
    blocks_ref,
    c0_ref,
    c1_ref,
    c2_ref,
    c3_ref,
    out_ref,
    grad_ref,
    x_ref,
    weight_ref,
    context_ref,
    c_ref,
    x_sems,
    sems,
    c_sems,
    out_sem,
):
    scale = HEAD**-0.5 * math.log2(math.e)
    hidden = -1e30 * HEAD**0.5
    copies = []
    for slot in range(12):
        source = blocks_ref.at[order_ref[16 * half_of(place_ref) + slot]]
        copies.append(pltpu.make_async_copy(source, weight_ref.at[slot * HEAD : (slot + 1) * HEAD], sems.at[slot]))
    arrivals = [
        pltpu.make_async_copy(ref, x_ref.at[part], x_sems.at[part])
        for part, ref in enumerate((x0_ref, x1_ref, x2_ref, x3_ref))
    ]
    cotangents = [
        pltpu.make_async_copy(ref, c_ref.at[part * ROWS : (part + 1) * ROWS], c_sems.at[part])
        for part, ref in enumerate((c0_ref, c1_ref, c2_ref, c3_ref))
    ]
    for copy in copies + arrivals + cotangents:
        copy.start()
    for copy in copies + arrivals:
        copy.wait()
    everything = [
        lax.dot_general(
            weight_ref[...], x_ref[part, :ROWS, :], (((1,), (1,)), ((), ())), preferred_element_type=F32
        ).astype(BF16)
        for part in range(4)
    ]
    for part in range(4):
        mixed = everything[part]
        code = x_ref[part, ROWS:, :ROWS].astype(F32)[0:1, :]
        square = jnp.broadcast_to(code, (ROWS, ROWS))
        allowed = square == square.T
        alive = code < 64.0
        def piece(kind, head):
            return mixed[(4 * kind + head) * HEAD : (4 * kind + head + 1) * HEAD, :]

        scores = [
            lax.dot_general(piece(1, head), piece(0, head), (((0,), (0,)), ((), ())), preferred_element_type=F32)
            for head in range(4)
        ]
        weights, totals = [], []
        for head in range(4):
            masked = jnp.where(allowed, scores[head], hidden)
            peak = jnp.max(masked, axis=0, keepdims=True)
            weight = jnp.exp2((masked - peak) * scale)
            totals.append(jnp.sum(weight, axis=0, keepdims=True))
            weights.append(weight.astype(BF16))
        for head in range(4):
            context = jnp.dot(piece(2, head), weights[head], preferred_element_type=F32)
            context = jnp.where(alive, context / totals[head], 0.0)
            context_ref[head * HEAD : (head + 1) * HEAD, part * ROWS : (part + 1) * ROWS] = context.astype(BF16)
    store = pltpu.make_async_copy(context_ref, out_ref, out_sem)
    store.start()
    for copy in cotangents:
        copy.wait()
    for start in range(0, WIDTH, 256):
        columns = slice(start, start + 256)
        grad_ref[:, columns] = jnp.dot(
            context_ref[...], c_ref[:, columns], preferred_element_type=F32
        ).astype(BF16)
    store.wait()


def project_kernel(
    place_ref, order_ref, from_ref, blocks_ref, keep_ref, send_ref, context_ref, held_ref, weight_ref, sems, sem, out_sems
):
    copies = [pltpu.make_async_copy(from_ref, context_ref, sem)]
    copies[0].start()
    for slot in range(4):
        source = blocks_ref.at[order_ref[16 * half_of(place_ref) + 12 + slot]]
        copies.append(pltpu.make_async_copy(source, weight_ref.at[slot * HEAD : (slot + 1) * HEAD], sems.at[slot]))
        copies[-1].start()
    for copy in copies:
        copy.wait()
    stores = []
    for part in (1, 3, 0, 2):
        projected = lax.dot_general(
            context_ref[:, part * ROWS : (part + 1) * ROWS],
            weight_ref[...],
            (((0,), (0,)), ((), ())),
            preferred_element_type=F32,
        )
        held_ref[part] = projected.astype(BF16)
        target = send_ref if part % 2 else keep_ref
        stores.append(pltpu.make_async_copy(held_ref.at[part], target.at[part // 2], out_sems.at[part]))
        stores[-1].start()
    for store in stores:
        store.wait()


def sum_kernel(terms_ref, copies_ref):
    total = terms_ref[0].astype(F32)
    for i in range(1, terms_ref.shape[0]):
        total = total + terms_ref[i].astype(F32)
    total = total.astype(BF16)
    for i in range(copies_ref.shape[0]):
        copies_ref[i] = total


VMEM = pl.BlockSpec(memory_space=pltpu.VMEM)
SMEM = pl.BlockSpec(memory_space=pltpu.SMEM)
HBM = pl.BlockSpec(memory_space=pltpu.HBM)
DMA = pltpu.SemaphoreType.DMA


def call(kernel, out_shape, in_specs, out_specs, scratch=(), limit=60 << 20, flops=0, read=0):
    return pl.pallas_call(
        kernel,
        out_shape=out_shape,
        in_specs=in_specs,
        out_specs=out_specs,
        scratch_shapes=scratch,
        compiler_params=pltpu.CompilerParams(vmem_limit_bytes=limit),
        cost_estimate=pl.CostEstimate(flops=flops, bytes_accessed=read, transcendentals=0),
    )


def array(*shape):
    return jax.ShapeDtypeStruct(shape, BF16)


def sum_of(terms, copies):
    return call(
        sum_kernel,
        array(copies, *terms.shape[1:]),
        [VMEM],
        VMEM,
        limit=16 << 20,
        read=2 * (copies + terms.shape[0]) * 40 * WIDTH
    )(terms)


def shards(patches, ln_gain, qkv_weight, proj_weight, out_cotangent, tile_counts, segment_ids):
    core = lax.axis_index("core")
    half = lax.axis_index("z_pair")
    x = lax.axis_index("x")
    shard = lax.axis_index("y_lo") * 4 + x
    place = lax.axis_index(AXES).reshape(1)
    sends, orders = jnp.asarray(SENDS), jnp.asarray(ORDERS)

    def to_core(value):
        return lax.ppermute(value, "core", CORE_SWAP)

    def to_pair(value):
        return lax.ppermute(value, "z_pair", PAIR_SWAP)

    message, own = call(
        front_kernel,
        (array(ROWS + NOTE, WIDTH), array(8, 2, HEAD, WIDTH)),
        [SMEM, SMEM, SMEM, HBM, VMEM, VMEM, HBM, HBM],
        (HBM, HBM),
        [
            pltpu.VMEM((ROWS, WIDTH), BF16),
            pltpu.VMEM((ROWS + NOTE, WIDTH), BF16),
            pltpu.VMEM((2, HEAD, WIDTH), BF16),
            DMA((2,)),
            DMA((16,)),
            DMA((2,)),
        ],
        read=6 << 20,
    )(
        place,
        sends,
        tile_counts,
        patches,
        ln_gain,
        segment_ids,
        qkv_weight.T.reshape(6, HEAD, WIDTH),
        proj_weight.reshape(2, HEAD, WIDTH),
    )
    blocks = lax.all_to_all(own, FSDP, 0, 0).reshape(16, HEAD, WIDTH)

    message_pair = to_pair(message)
    cotangent_pair = to_pair(out_cotangent)
    message_core = to_core(message)
    cotangent_core = to_core(out_cotangent)
    message_both = to_core(message_pair)
    cotangent_both = to_core(cotangent_pair)

    context, grad = call(
        attention_kernel,
        (array(4 * HEAD, 4 * ROWS), array(4 * HEAD, WIDTH)),
        [SMEM, SMEM] + [HBM] * 9,
        (HBM, VMEM),
        [
            pltpu.VMEM((4, ROWS + NOTE, WIDTH), BF16),
            pltpu.VMEM((12 * HEAD, WIDTH), BF16),
            pltpu.VMEM((4 * HEAD, 4 * ROWS), BF16),
            pltpu.VMEM((4 * ROWS, WIDTH), BF16),
            DMA((4,)),
            DMA((12,)),
            DMA((4,)),
            DMA,
        ],
        limit=52 << 20,
        flops=2 * 1024 * 1280 * 1280 + 4 * 16 * 256 * 256 * 128,
        read=12 << 20,
    )(
        place,
        orders,
        message,
        message_core,
        message_pair,
        message_both,
        blocks,
        out_cotangent,
        cotangent_core,
        cotangent_pair,
        cotangent_both,
    )

    keep_out, send_out = call(
        project_kernel,
        (array(2, ROWS, WIDTH), array(2, ROWS, WIDTH)),
        [SMEM, SMEM, HBM, HBM],
        (HBM, HBM),
        [
            pltpu.VMEM((4 * HEAD, 4 * ROWS), BF16),
            pltpu.VMEM((4, ROWS, WIDTH), BF16),
            pltpu.VMEM((4 * HEAD, WIDTH), BF16),
            DMA((4,)),
            DMA,
            DMA((4,)),
        ],
        limit=52 << 20,
        flops=2 * 1024 * 1280 * 320,
        read=6 << 20,
    )(place, orders, context, blocks)

    grad = lax.all_to_all(grad.reshape(8, 40, WIDTH), FSDP, 0, 0)
    grad, keep_late = lax.optimization_barrier((grad, keep_out))
    grad = sum_of(grad, Z_QUAD)
    from_core = to_core(send_out)
    for_pair = (keep_out[1].astype(F32) + from_core[1].astype(F32)).astype(BF16)
    grad = lax.all_to_all(grad, ("y_hi", "z_quad", "core"), 0, 0, axis_index_groups=cross_groups(0))
    grad, from_core_late = lax.optimization_barrier((grad, from_core))
    grad = sum_of(grad, Y_HI)
    from_pair = to_pair(for_pair)
    grad = lax.all_to_all(grad, ("y_hi", "z_quad", "core"), 0, 0, axis_index_groups=cross_groups(1))
    grad, from_pair = lax.optimization_barrier((grad, from_pair))
    grad = sum_of(grad, 1)[0]

    first = lax.ppermute(grad, ("x", "z_pair"), TO_OWNER)
    second = lax.ppermute(grad, ("x", "z_pair"), ACROSS)
    projected = keep_late[0].astype(F32) + from_core_late[0].astype(F32) + from_pair.astype(F32)
    alive = lax.iota(jnp.int32, ROWS) < tile_counts[0] * TILE
    output = jnp.where(alive[:, None], patches.astype(F32) + projected, F32(0.0)).astype(BF16)
    second, output = lax.optimization_barrier((second, output))
    owner = ((x == 0) | (x == 3)) == (half == 1)
    two = lax.broadcasted_iota(jnp.int32, (2, 1, 1), 0)
    head_grad = jnp.where(two == x % 2, jnp.where(owner, grad, first), jnp.where(owner, first, second))
    head_grad = head_grad.reshape(HEAD, WIDTH)
    proj_grad = jnp.where(two == core, head_grad, to_core(head_grad)).reshape(2 * HEAD, WIDTH)
    return output, proj_grad


def solution(mesh):
    fine = Mesh(mesh.devices.reshape(2, 4, Y_HI, Z_QUAD, Z_PAIR, CORES), AXES)
    return jax.shard_map(
        shards,
        mesh=fine,
        in_specs=(P(AXES, None), P(), P(None, FSDP), P(FSDP, None), P(AXES, None), P(AXES), P(AXES)),
        out_specs=(P(AXES, None), P(FSDP, None)),
        check_vma=False,
    )
```

```python
import math

import jax
import jax.numpy as jnp
import numpy as np
from jax import lax
from jax.experimental import pallas as pl
from jax.experimental.pallas import tpu as pltpu
from jax.sharding import Mesh
from jax.sharding import PartitionSpec as P

HEADS = 16
HEAD = 80
TILE = 128
ROWS = 256
NOTE = 16
WIDTH = 1280
EPSILON = 1e-06
BF16 = jnp.bfloat16
F32 = jnp.float32

Y_HI, Z_QUAD, Z_PAIR, CORES = 4, 4, 2, 2
AXES = ("y_lo", "x", "y_hi", "z_quad", "z_pair", "core")
FSDP = ("y_lo", "x")

HEAD_SETS = ((1, 2, 5, 6), (0, 3, 4, 7))


def block_tables():
    sends = np.zeros((8, 2, 2), np.int32)
    orders = np.zeros((2, 16), np.int32)
    for half, heads in enumerate(HEAD_SETS):
        for shard in range(8):
            picked = [k for k in range(3) if (3 * shard + k) % 8 in heads] + ([3] if shard in heads else [])
            assert len(picked) == 2
            for place, k in enumerate(picked):
                sends[shard, half, place] = k
                if k == 3:
                    slot = 12 + heads.index(shard)
                else:
                    kind, m = divmod(3 * shard + k, 8)
                    slot = 4 * kind + heads.index(m)
                orders[half, slot] = 2 * shard + place
    return sends.reshape(-1), orders.reshape(-1)


SENDS, ORDERS = block_tables()


def owns(x, half):
    return int(x in (0, 3)) == half


CORE_SWAP = [(0, 1), (1, 0)]
PAIR_SWAP = [(0, 1), (1, 0)]
TO_OWNER = [
    (2 * x + half, 2 * x + (1 - half) if owns(x, half) else 2 * (x ^ 1) + half) for x in range(4) for half in range(2)
]
ACROSS = [(2 * x + half, 2 * (x ^ 1) + (1 - half)) for x in range(4) for half in range(2) if not owns(x, half)]


CROSS = ("y_lo", "y_hi", "z_quad", "z_pair", "core")


def cross_groups(first):
    def place(y_lo, y, z, half, core):
        return (((y_lo * Y_HI + y % Y_HI) * Z_QUAD + z % Z_QUAD) * Z_PAIR + half) * CORES + core

    groups = []
    for y_lo in range(2):
        for half in range(Z_PAIR):
            for other in range(4):
                groups.append([place(y_lo, other, z + 2 * half, half, first) for z in range(Z_QUAD)])
                groups.append([place(y_lo, y + 2 * y_lo, other, half, 1 - first) for y in range(Y_HI)])
    return groups


def half_of(place_ref):
    return place_ref[0] // CORES % Z_PAIR


def front_kernel(
    place_ref,
    sends_ref,
    count_ref,
    patches_ref,
    gain_ref,
    images_ref,
    qkv_ref,
    proj_ref,
    out_ref,
    blocks_ref,
    rows_ref,
    message_ref,
    held_ref,
    read_sems,
    write_sems,
    sems,
):
    shard = place_ref[0] // (Y_HI * Z_QUAD * Z_PAIR * CORES)
    core = place_ref[0] % CORES
    for i in range(2):
        choice = sends_ref[4 * shard + 2 * half_of(place_ref) + i]

        @pl.when(choice < 3)
        def _():
            pltpu.make_async_copy(qkv_ref.at[2 * jnp.minimum(choice, 2) + core], held_ref.at[i], read_sems.at[i]).start()

        @pl.when(choice == 3)
        def _():
            pltpu.make_async_copy(proj_ref.at[core], held_ref.at[i], read_sems.at[i]).start()

    fetch = pltpu.make_async_copy(patches_ref, rows_ref, sems.at[0])
    fetch.start()
    copies = []
    for i in range(2):
        pltpu.make_async_copy(proj_ref.at[0], held_ref.at[i], read_sems.at[i]).wait()
        for peer in range(8):
            copies.append(pltpu.make_async_copy(held_ref.at[i], blocks_ref.at[peer, i], write_sems.at[8 * i + peer]))
            copies[-1].start()

    fetch.wait()
    inputs = rows_ref[...].astype(F32)
    row_mean = jnp.mean(inputs, axis=1, keepdims=True)
    centred = inputs - row_mean
    variance = jnp.mean(centred * centred, axis=1, keepdims=True)
    message_ref[:ROWS, :] = (centred * lax.rsqrt(variance + EPSILON) * gain_ref[...].reshape(1, WIDTH)).astype(BF16)
    dead = lax.broadcasted_iota(jnp.int32, (1, ROWS), 1) >= count_ref[0] * TILE
    code = (images_ref[...].reshape(1, ROWS) + jnp.where(dead, 64, 0)).astype(F32)
    message_ref[ROWS:, :] = jnp.zeros((NOTE, WIDTH), BF16)
    message_ref[ROWS:, :ROWS] = jnp.broadcast_to(code, (NOTE, ROWS)).astype(BF16)
    copies.append(pltpu.make_async_copy(message_ref, out_ref, sems.at[1]))
    copies[-1].start()
    for copy in copies:
        copy.wait()


def attention_kernel(
    place_ref,
    order_ref,
    x0_ref,
    x1_ref,
    x2_ref,
    x3_ref,
    blocks_ref,
    c0_ref,
    c1_ref,
    c2_ref,
    c3_ref,
    out_ref,
    grad_ref,
    x_ref,
    weight_ref,
    context_ref,
    c_ref,
    x_sems,
    sems,
    c_sems,
    out_sem,
):
    scale = HEAD**-0.5 * math.log2(math.e)
    hidden = -1e30 * HEAD**0.5
    copies = []
    for slot in range(12):
        source = blocks_ref.at[order_ref[16 * half_of(place_ref) + slot]]
        copies.append(pltpu.make_async_copy(source, weight_ref.at[slot * HEAD : (slot + 1) * HEAD], sems.at[slot]))
    arrivals = [
        pltpu.make_async_copy(ref, x_ref.at[part], x_sems.at[part])
        for part, ref in enumerate((x0_ref, x1_ref, x2_ref, x3_ref))
    ]
    cotangents = [
        pltpu.make_async_copy(ref, c_ref.at[part * ROWS : (part + 1) * ROWS], c_sems.at[part])
        for part, ref in enumerate((c0_ref, c1_ref, c2_ref, c3_ref))
    ]
    for copy in copies + arrivals + cotangents:
        copy.start()
    for copy in copies + arrivals:
        copy.wait()
    everything = [
        lax.dot_general(
            weight_ref[...], x_ref[part, :ROWS, :], (((1,), (1,)), ((), ())), preferred_element_type=F32
        ).astype(BF16)
        for part in range(4)
    ]
    for part in range(4):
        mixed = everything[part]
        code = x_ref[part, ROWS:, :ROWS].astype(F32)[0:1, :]
        square = jnp.broadcast_to(code, (ROWS, ROWS))
        allowed = square == square.T
        alive = code < 64.0
        def piece(kind, head):
            return mixed[(4 * kind + head) * HEAD : (4 * kind + head + 1) * HEAD, :]

        scores = [
            lax.dot_general(piece(1, head), piece(0, head), (((0,), (0,)), ((), ())), preferred_element_type=F32)
            for head in range(4)
        ]
        weights, totals = [], []
        for head in range(4):
            masked = jnp.where(allowed, scores[head], hidden)
            peak = jnp.max(masked, axis=0, keepdims=True)
            weight = jnp.exp2((masked - peak) * scale)
            totals.append(jnp.sum(weight, axis=0, keepdims=True))
            weights.append(weight.astype(BF16))
        for head in range(4):
            context = jnp.dot(piece(2, head), weights[head], preferred_element_type=F32)
            context = jnp.where(alive, context / totals[head], 0.0)
            context_ref[head * HEAD : (head + 1) * HEAD, part * ROWS : (part + 1) * ROWS] = context.astype(BF16)
    store = pltpu.make_async_copy(context_ref, out_ref, out_sem)
    store.start()
    for copy in cotangents:
        copy.wait()
    for start in range(0, WIDTH, 256):
        columns = slice(start, start + 256)
        grad_ref[:, columns] = jnp.dot(
            context_ref[...], c_ref[:, columns], preferred_element_type=F32
        ).astype(BF16)
    store.wait()


def project_kernel(
    place_ref, order_ref, from_ref, blocks_ref, keep_ref, send_ref, context_ref, held_ref, weight_ref, sems, sem, out_sems
):
    copies = [pltpu.make_async_copy(from_ref, context_ref, sem)]
    copies[0].start()
    for slot in range(4):
        source = blocks_ref.at[order_ref[16 * half_of(place_ref) + 12 + slot]]
        copies.append(pltpu.make_async_copy(source, weight_ref.at[slot * HEAD : (slot + 1) * HEAD], sems.at[slot]))
        copies[-1].start()
    for copy in copies:
        copy.wait()
    stores = []
    for part in (1, 3, 0, 2):
        projected = lax.dot_general(
            context_ref[:, part * ROWS : (part + 1) * ROWS],
            weight_ref[...],
            (((0,), (0,)), ((), ())),
            preferred_element_type=F32,
        )
        held_ref[part] = projected.astype(BF16)
        target = send_ref if part % 2 else keep_ref
        stores.append(pltpu.make_async_copy(held_ref.at[part], target.at[part // 2], out_sems.at[part]))
        stores[-1].start()
    for store in stores:
        store.wait()


def sum_kernel(terms_ref, copies_ref):
    total = terms_ref[0].astype(F32)
    for i in range(1, terms_ref.shape[0]):
        total = total + terms_ref[i].astype(F32)
    total = total.astype(BF16)
    for i in range(copies_ref.shape[0]):
        copies_ref[i] = total


VMEM = pl.BlockSpec(memory_space=pltpu.VMEM)
SMEM = pl.BlockSpec(memory_space=pltpu.SMEM)
HBM = pl.BlockSpec(memory_space=pltpu.HBM)
DMA = pltpu.SemaphoreType.DMA


def call(kernel, out_shape, in_specs, out_specs, scratch=(), limit=60 << 20, flops=0, read=0):
    return pl.pallas_call(
        kernel,
        out_shape=out_shape,
        in_specs=in_specs,
        out_specs=out_specs,
        scratch_shapes=scratch,
        compiler_params=pltpu.CompilerParams(vmem_limit_bytes=limit),
        cost_estimate=pl.CostEstimate(flops=flops, bytes_accessed=read, transcendentals=0),
    )


def array(*shape):
    return jax.ShapeDtypeStruct(shape, BF16)


def sum_of(terms, copies):
    return call(
        sum_kernel,
        array(copies, *terms.shape[1:]),
        [VMEM],
        VMEM,
        limit=16 << 20,
        read=2 * (copies + terms.shape[0]) * 40 * WIDTH
    )(terms)


def shards(patches, ln_gain, qkv_weight, proj_weight, out_cotangent, tile_counts, segment_ids):
    core = lax.axis_index("core")
    half = lax.axis_index("z_pair")
    x = lax.axis_index("x")
    shard = lax.axis_index("y_lo") * 4 + x
    place = lax.axis_index(AXES).reshape(1)
    sends, orders = jnp.asarray(SENDS), jnp.asarray(ORDERS)

    def to_core(value):
        return lax.ppermute(value, "core", CORE_SWAP)

    def to_pair(value):
        return lax.ppermute(value, "z_pair", PAIR_SWAP)

    message, own = call(
        front_kernel,
        (array(ROWS + NOTE, WIDTH), array(8, 2, HEAD, WIDTH)),
        [SMEM, SMEM, SMEM, HBM, VMEM, VMEM, HBM, HBM],
        (HBM, HBM),
        [
            pltpu.VMEM((ROWS, WIDTH), BF16),
            pltpu.VMEM((ROWS + NOTE, WIDTH), BF16),
            pltpu.VMEM((2, HEAD, WIDTH), BF16),
            DMA((2,)),
            DMA((16,)),
            DMA((2,)),
        ],
        read=6 << 20,
    )(
        place,
        sends,
        tile_counts,
        patches,
        ln_gain,
        segment_ids,
        qkv_weight.T.reshape(6, HEAD, WIDTH),
        proj_weight.reshape(2, HEAD, WIDTH),
    )
    blocks = lax.all_to_all(own, FSDP, 0, 0).reshape(16, HEAD, WIDTH)

    message_pair = to_pair(message)
    cotangent_pair = to_pair(out_cotangent)
    message_core = to_core(message)
    cotangent_core = to_core(out_cotangent)
    message_both = to_core(message_pair)
    cotangent_both = to_core(cotangent_pair)

    context, grad = call(
        attention_kernel,
        (array(4 * HEAD, 4 * ROWS), array(4 * HEAD, WIDTH)),
        [SMEM, SMEM] + [HBM] * 9,
        (HBM, VMEM),
        [
            pltpu.VMEM((4, ROWS + NOTE, WIDTH), BF16),
            pltpu.VMEM((12 * HEAD, WIDTH), BF16),
            pltpu.VMEM((4 * HEAD, 4 * ROWS), BF16),
            pltpu.VMEM((4 * ROWS, WIDTH), BF16),
            DMA((4,)),
            DMA((12,)),
            DMA((4,)),
            DMA,
        ],
        limit=52 << 20,
        flops=2 * 1024 * 1280 * 1280 + 4 * 16 * 256 * 256 * 128,
        read=12 << 20,
    )(
        place,
        orders,
        message,
        message_core,
        message_pair,
        message_both,
        blocks,
        out_cotangent,
        cotangent_core,
        cotangent_pair,
        cotangent_both,
    )

    keep_out, send_out = call(
        project_kernel,
        (array(2, ROWS, WIDTH), array(2, ROWS, WIDTH)),
        [SMEM, SMEM, HBM, HBM],
        (HBM, HBM),
        [
            pltpu.VMEM((4 * HEAD, 4 * ROWS), BF16),
            pltpu.VMEM((4, ROWS, WIDTH), BF16),
            pltpu.VMEM((4 * HEAD, WIDTH), BF16),
            DMA((4,)),
            DMA,
            DMA((4,)),
        ],
        limit=52 << 20,
        flops=2 * 1024 * 1280 * 320,
        read=6 << 20,
    )(place, orders, context, blocks)

    grad = lax.all_to_all(grad.reshape(8, 40, WIDTH), FSDP, 0, 0)
    grad, keep_late = lax.optimization_barrier((grad, keep_out))
    grad = sum_of(grad, Z_QUAD)
    from_core = to_core(send_out)
    for_pair = (keep_out[1].astype(F32) + from_core[1].astype(F32)).astype(BF16)
    grad = lax.all_to_all(grad, CROSS, 0, 0, axis_index_groups=cross_groups(0))
    grad, from_core_late = lax.optimization_barrier((grad, from_core))
    grad = sum_of(grad, Y_HI)
    from_pair = to_pair(for_pair)
    grad = lax.all_to_all(grad, CROSS, 0, 0, axis_index_groups=cross_groups(1))
    grad, from_pair = lax.optimization_barrier((grad, from_pair))
    grad = sum_of(grad, 1)[0]

    first = lax.ppermute(grad, ("x", "z_pair"), TO_OWNER)
    second = lax.ppermute(grad, ("x", "z_pair"), ACROSS)
    projected = keep_late[0].astype(F32) + from_core_late[0].astype(F32) + from_pair.astype(F32)
    alive = lax.iota(jnp.int32, ROWS) < tile_counts[0] * TILE
    output = jnp.where(alive[:, None], patches.astype(F32) + projected, F32(0.0)).astype(BF16)
    second, output = lax.optimization_barrier((second, output))
    owner = ((x == 0) | (x == 3)) == (half == 1)
    two = lax.broadcasted_iota(jnp.int32, (2, 1, 1), 0)
    head_grad = jnp.where(two == x % 2, jnp.where(owner, grad, first), jnp.where(owner, first, second))
    head_grad = head_grad.reshape(HEAD, WIDTH)
    proj_grad = jnp.where(two == core, head_grad, to_core(head_grad)).reshape(2 * HEAD, WIDTH)
    return output, proj_grad


def solution(mesh):
    fine = Mesh(mesh.devices.reshape(2, 4, Y_HI, Z_QUAD, Z_PAIR, CORES), AXES)
    return jax.shard_map(
        shards,
        mesh=fine,
        in_specs=(P(AXES, None), P(), P(None, FSDP), P(FSDP, None), P(AXES, None), P(AXES), P(AXES)),
        out_specs=(P(AXES, None), P(FSDP, None)),
        check_vma=False,
    )
```

```python
import math

import jax
import jax.numpy as jnp
import numpy as np
from jax import lax
from jax.experimental import pallas as pl
from jax.experimental.pallas import tpu as pltpu
from jax.sharding import Mesh
from jax.sharding import PartitionSpec as P

HEADS = 16
HEAD = 80
TILE = 128
ROWS = 256
NOTE = 16
WIDTH = 1280
EPSILON = 1e-06
BF16 = jnp.bfloat16
F32 = jnp.float32

Y_HI, Z_QUAD, Z_PAIR, CORES = 4, 4, 2, 2
AXES = ("y_lo", "x", "y_hi", "z_quad", "z_pair", "core")
FSDP = ("y_lo", "x")

HEAD_SETS = ((1, 2, 5, 6), (0, 3, 4, 7))


def rank_of(shard, core):
    return 2 * (3 - shard // 2) + shard % 2 if core else shard


def block_tables():
    sends = np.zeros((8, 2, 2), np.int32)
    orders = np.zeros((2, 2, 16), np.int32)
    for half, heads in enumerate(HEAD_SETS):
        for shard in range(8):
            picked = [k for k in range(3) if (3 * shard + k) % 8 in heads] + ([3] if shard in heads else [])
            assert len(picked) == 2
            for place, k in enumerate(picked):
                sends[shard, half, place] = k
                kind, m = (3, shard) if k == 3 else divmod(3 * shard + k, 8)
                for core in range(2):
                    listed = heads[::-1] if core else heads
                    orders[half, core, 4 * kind + listed.index(m)] = 2 * rank_of(shard, core) + place
    return sends.reshape(-1), orders.reshape(-1)


SENDS, ORDERS = block_tables()


def owns(x, half):
    return int(x in (0, 3)) == half


CORE_SWAP = [(0, 1), (1, 0)]
PAIR_SWAP = [(0, 1), (1, 0)]
TO_OWNER = [
    (2 * x + half, 2 * x + (1 - half) if owns(x, half) else 2 * (x ^ 1) + half) for x in range(4) for half in range(2)
]
ACROSS = [(2 * x + half, 2 * (x ^ 1) + (1 - half)) for x in range(4) for half in range(2) if not owns(x, half)]


SHARDS = ("y_lo", "x", "core")
SHARD_GROUPS = [[rank_of(rank, core) * CORES + core for rank in range(8)] for core in range(CORES)]
CROSS = ("y_lo", "y_hi", "z_quad", "z_pair", "core")


def cross_groups(first):
    def place(y_lo, y, z, half, core):
        return (((y_lo * Y_HI + y % Y_HI) * Z_QUAD + z % Z_QUAD) * Z_PAIR + half) * CORES + core

    groups = []
    for y_lo in range(2):
        for half in range(Z_PAIR):
            for other in range(4):
                groups.append([place(y_lo, other, z + 2 * half, half, first) for z in range(Z_QUAD)])
                groups.append([place(y_lo, y + 2 * y_lo, other, half, 1 - first) for y in range(Y_HI)])
    return groups


def half_of(place_ref):
    return place_ref[0] // CORES % Z_PAIR


def front_kernel(
    place_ref,
    sends_ref,
    count_ref,
    patches_ref,
    gain_ref,
    images_ref,
    qkv_ref,
    proj_ref,
    out_ref,
    blocks_ref,
    rows_ref,
    message_ref,
    held_ref,
    read_sems,
    write_sems,
    sems,
):
    shard = place_ref[0] // (Y_HI * Z_QUAD * Z_PAIR * CORES)
    core = place_ref[0] % CORES
    for i in range(2):
        choice = sends_ref[4 * shard + 2 * half_of(place_ref) + i]

        @pl.when(choice < 3)
        def _():
            pltpu.make_async_copy(qkv_ref.at[2 * jnp.minimum(choice, 2) + core], held_ref.at[i], read_sems.at[i]).start()

        @pl.when(choice == 3)
        def _():
            pltpu.make_async_copy(proj_ref.at[core], held_ref.at[i], read_sems.at[i]).start()

    fetch = pltpu.make_async_copy(patches_ref, rows_ref, sems.at[0])
    fetch.start()
    copies = []
    for i in range(2):
        pltpu.make_async_copy(proj_ref.at[0], held_ref.at[i], read_sems.at[i]).wait()
        for peer in range(8):
            copies.append(pltpu.make_async_copy(held_ref.at[i], blocks_ref.at[peer, i], write_sems.at[8 * i + peer]))
            copies[-1].start()

    fetch.wait()
    inputs = rows_ref[...].astype(F32)
    row_mean = jnp.mean(inputs, axis=1, keepdims=True)
    centred = inputs - row_mean
    variance = jnp.mean(centred * centred, axis=1, keepdims=True)
    message_ref[:ROWS, :] = (centred * lax.rsqrt(variance + EPSILON) * gain_ref[...].reshape(1, WIDTH)).astype(BF16)
    dead = lax.broadcasted_iota(jnp.int32, (1, ROWS), 1) >= count_ref[0] * TILE
    code = (images_ref[...].reshape(1, ROWS) + jnp.where(dead, 64, 0)).astype(F32)
    message_ref[ROWS:, :] = jnp.zeros((NOTE, WIDTH), BF16)
    message_ref[ROWS:, :ROWS] = jnp.broadcast_to(code, (NOTE, ROWS)).astype(BF16)
    copies.append(pltpu.make_async_copy(message_ref, out_ref, sems.at[1]))
    copies[-1].start()
    for copy in copies:
        copy.wait()


def attention_kernel(
    place_ref,
    order_ref,
    x0_ref,
    x1_ref,
    x2_ref,
    x3_ref,
    blocks_ref,
    c0_ref,
    c1_ref,
    c2_ref,
    c3_ref,
    out_ref,
    grad_ref,
    x_ref,
    weight_ref,
    context_ref,
    c_ref,
    x_sems,
    sems,
    c_sems,
    out_sem,
):
    scale = HEAD**-0.5 * math.log2(math.e)
    hidden = -1e30 * HEAD**0.5
    copies = []
    for slot in range(12):
        source = blocks_ref.at[order_ref[16 * (place_ref[0] % 4) + slot]]
        copies.append(pltpu.make_async_copy(source, weight_ref.at[slot * HEAD : (slot + 1) * HEAD], sems.at[slot]))
    arrivals = [
        pltpu.make_async_copy(ref, x_ref.at[part], x_sems.at[part])
        for part, ref in enumerate((x0_ref, x1_ref, x2_ref, x3_ref))
    ]
    cotangents = [
        pltpu.make_async_copy(ref, c_ref.at[part * ROWS : (part + 1) * ROWS], c_sems.at[part])
        for part, ref in enumerate((c0_ref, c1_ref, c2_ref, c3_ref))
    ]
    for copy in copies + arrivals + cotangents:
        copy.start()
    for copy in copies + arrivals:
        copy.wait()
    everything = [
        lax.dot_general(
            weight_ref[...], x_ref[part, :ROWS, :], (((1,), (1,)), ((), ())), preferred_element_type=F32
        ).astype(BF16)
        for part in range(4)
    ]
    for part in range(4):
        mixed = everything[part]
        code = x_ref[part, ROWS:, :ROWS].astype(F32)[0:1, :]
        square = jnp.broadcast_to(code, (ROWS, ROWS))
        allowed = square == square.T
        alive = code < 64.0
        def piece(kind, head):
            return mixed[(4 * kind + head) * HEAD : (4 * kind + head + 1) * HEAD, :]

        scores = [
            lax.dot_general(piece(1, head), piece(0, head), (((0,), (0,)), ((), ())), preferred_element_type=F32)
            for head in range(4)
        ]
        weights, totals = [], []
        for head in range(4):
            masked = jnp.where(allowed, scores[head], hidden)
            peak = jnp.max(masked, axis=0, keepdims=True)
            weight = jnp.exp2((masked - peak) * scale)
            totals.append(jnp.sum(weight, axis=0, keepdims=True))
            weights.append(weight.astype(BF16))
        for head in range(4):
            context = jnp.dot(piece(2, head), weights[head], preferred_element_type=F32)
            context = jnp.where(alive, context / totals[head], 0.0)
            context_ref[head * HEAD : (head + 1) * HEAD, part * ROWS : (part + 1) * ROWS] = context.astype(BF16)
    store = pltpu.make_async_copy(context_ref, out_ref, out_sem)
    store.start()
    for copy in cotangents:
        copy.wait()
    for start in range(0, WIDTH, 256):
        columns = slice(start, start + 256)
        grad_ref[:, columns] = jnp.dot(
            context_ref[...], c_ref[:, columns], preferred_element_type=F32
        ).astype(BF16)
    store.wait()


def project_kernel(
    place_ref, order_ref, from_ref, blocks_ref, keep_ref, send_ref, context_ref, held_ref, weight_ref, sems, sem, out_sems
):
    copies = [pltpu.make_async_copy(from_ref, context_ref, sem)]
    copies[0].start()
    for slot in range(4):
        source = blocks_ref.at[order_ref[16 * (place_ref[0] % 4) + 12 + slot]]
        copies.append(pltpu.make_async_copy(source, weight_ref.at[slot * HEAD : (slot + 1) * HEAD], sems.at[slot]))
        copies[-1].start()
    for copy in copies:
        copy.wait()
    stores = []
    for part in (1, 3, 0, 2):
        projected = lax.dot_general(
            context_ref[:, part * ROWS : (part + 1) * ROWS],
            weight_ref[...],
            (((0,), (0,)), ((), ())),
            preferred_element_type=F32,
        )
        held_ref[part] = projected.astype(BF16)
        target = send_ref if part % 2 else keep_ref
        stores.append(pltpu.make_async_copy(held_ref.at[part], target.at[part // 2], out_sems.at[part]))
        stores[-1].start()
    for store in stores:
        store.wait()


def sum_kernel(terms_ref, copies_ref):
    total = terms_ref[0].astype(F32)
    for i in range(1, terms_ref.shape[0]):
        total = total + terms_ref[i].astype(F32)
    total = total.astype(BF16)
    for i in range(copies_ref.shape[0]):
        copies_ref[i] = total


VMEM = pl.BlockSpec(memory_space=pltpu.VMEM)
SMEM = pl.BlockSpec(memory_space=pltpu.SMEM)
HBM = pl.BlockSpec(memory_space=pltpu.HBM)
DMA = pltpu.SemaphoreType.DMA


def call(kernel, out_shape, in_specs, out_specs, scratch=(), limit=60 << 20, flops=0, read=0):
    return pl.pallas_call(
        kernel,
        out_shape=out_shape,
        in_specs=in_specs,
        out_specs=out_specs,
        scratch_shapes=scratch,
        compiler_params=pltpu.CompilerParams(vmem_limit_bytes=limit),
        cost_estimate=pl.CostEstimate(flops=flops, bytes_accessed=read, transcendentals=0),
    )


def array(*shape):
    return jax.ShapeDtypeStruct(shape, BF16)


def sum_of(terms, copies):
    return call(
        sum_kernel,
        array(copies, *terms.shape[1:]),
        [VMEM],
        VMEM,
        limit=16 << 20,
        read=2 * (copies + terms.shape[0]) * 40 * WIDTH
    )(terms)


def shards(patches, ln_gain, qkv_weight, proj_weight, out_cotangent, tile_counts, segment_ids):
    core = lax.axis_index("core")
    half = lax.axis_index("z_pair")
    x = lax.axis_index("x")
    shard = lax.axis_index("y_lo") * 4 + x
    place = lax.axis_index(AXES).reshape(1)
    sends, orders = jnp.asarray(SENDS), jnp.asarray(ORDERS)

    def to_core(value):
        return lax.ppermute(value, "core", CORE_SWAP)

    def to_pair(value):
        return lax.ppermute(value, "z_pair", PAIR_SWAP)

    message, own = call(
        front_kernel,
        (array(ROWS + NOTE, WIDTH), array(8, 2, HEAD, WIDTH)),
        [SMEM, SMEM, SMEM, HBM, VMEM, VMEM, HBM, HBM],
        (HBM, HBM),
        [
            pltpu.VMEM((ROWS, WIDTH), BF16),
            pltpu.VMEM((ROWS + NOTE, WIDTH), BF16),
            pltpu.VMEM((2, HEAD, WIDTH), BF16),
            DMA((2,)),
            DMA((16,)),
            DMA((2,)),
        ],
        read=6 << 20,
    )(
        place,
        sends,
        tile_counts,
        patches,
        ln_gain,
        segment_ids,
        qkv_weight.T.reshape(6, HEAD, WIDTH),
        proj_weight.reshape(2, HEAD, WIDTH),
    )
    blocks = lax.all_to_all(own, SHARDS, 0, 0, axis_index_groups=SHARD_GROUPS).reshape(16, HEAD, WIDTH)

    message_pair = to_pair(message)
    cotangent_pair = to_pair(out_cotangent)
    message_core = to_core(message)
    cotangent_core = to_core(out_cotangent)
    message_both = to_core(message_pair)
    cotangent_both = to_core(cotangent_pair)

    context, grad = call(
        attention_kernel,
        (array(4 * HEAD, 4 * ROWS), array(4 * HEAD, WIDTH)),
        [SMEM, SMEM] + [HBM] * 9,
        (HBM, VMEM),
        [
            pltpu.VMEM((4, ROWS + NOTE, WIDTH), BF16),
            pltpu.VMEM((12 * HEAD, WIDTH), BF16),
            pltpu.VMEM((4 * HEAD, 4 * ROWS), BF16),
            pltpu.VMEM((4 * ROWS, WIDTH), BF16),
            DMA((4,)),
            DMA((12,)),
            DMA((4,)),
            DMA,
        ],
        limit=52 << 20,
        flops=2 * 1024 * 1280 * 1280 + 4 * 16 * 256 * 256 * 128,
        read=12 << 20,
    )(
        place,
        orders,
        message,
        message_core,
        message_pair,
        message_both,
        blocks,
        out_cotangent,
        cotangent_core,
        cotangent_pair,
        cotangent_both,
    )

    keep_out, send_out = call(
        project_kernel,
        (array(2, ROWS, WIDTH), array(2, ROWS, WIDTH)),
        [SMEM, SMEM, HBM, HBM],
        (HBM, HBM),
        [
            pltpu.VMEM((4 * HEAD, 4 * ROWS), BF16),
            pltpu.VMEM((4, ROWS, WIDTH), BF16),
            pltpu.VMEM((4 * HEAD, WIDTH), BF16),
            DMA((4,)),
            DMA,
            DMA((4,)),
        ],
        limit=52 << 20,
        flops=2 * 1024 * 1280 * 320,
        read=6 << 20,
    )(place, orders, context, blocks)

    grad = lax.all_to_all(grad.reshape(8, 40, WIDTH), SHARDS, 0, 0, axis_index_groups=SHARD_GROUPS)
    grad, keep_late = lax.optimization_barrier((grad, keep_out))
    grad = sum_of(grad, Z_QUAD)
    from_core = to_core(send_out)
    for_pair = (keep_out[1].astype(F32) + from_core[1].astype(F32)).astype(BF16)
    grad = lax.all_to_all(grad, CROSS, 0, 0, axis_index_groups=cross_groups(0))
    grad, from_core_late = lax.optimization_barrier((grad, from_core))
    grad = sum_of(grad, Y_HI)
    from_pair = to_pair(for_pair)
    grad = lax.all_to_all(grad, CROSS, 0, 0, axis_index_groups=cross_groups(1))
    grad, from_pair = lax.optimization_barrier((grad, from_pair))
    grad = sum_of(grad, 1)[0]

    first = lax.ppermute(grad, ("x", "z_pair"), TO_OWNER)
    second = lax.ppermute(grad, ("x", "z_pair"), ACROSS)
    projected = keep_late[0].astype(F32) + from_core_late[0].astype(F32) + from_pair.astype(F32)
    alive = lax.iota(jnp.int32, ROWS) < tile_counts[0] * TILE
    output = jnp.where(alive[:, None], patches.astype(F32) + projected, F32(0.0)).astype(BF16)
    second, output = lax.optimization_barrier((second, output))
    owner = ((x == 0) | (x == 3)) == (half == 1)
    two = lax.broadcasted_iota(jnp.int32, (2, 1, 1), 0)
    head_grad = jnp.where(two == x % 2, jnp.where(owner, grad, first), jnp.where(owner, first, second))
    head_grad = head_grad.reshape(HEAD, WIDTH)
    proj_grad = jnp.where(two == core, head_grad, to_core(head_grad)).reshape(2 * HEAD, WIDTH)
    return output, proj_grad


def solution(mesh):
    fine = Mesh(mesh.devices.reshape(2, 4, Y_HI, Z_QUAD, Z_PAIR, CORES), AXES)
    return jax.shard_map(
        shards,
        mesh=fine,
        in_specs=(P(AXES, None), P(), P(None, FSDP), P(FSDP, None), P(AXES, None), P(AXES), P(AXES)),
        out_specs=(P(AXES, None), P(FSDP, None)),
        check_vma=False,
    )
```

```python
import math

import jax
import jax.numpy as jnp
import numpy as np
from jax import lax
from jax.experimental import pallas as pl
from jax.experimental.pallas import tpu as pltpu
from jax.sharding import Mesh
from jax.sharding import PartitionSpec as P

HEADS = 16
HEAD = 80
TILE = 128
ROWS = 256
NOTE = 16
WIDTH = 1280
EPSILON = 1e-06
BF16 = jnp.bfloat16
F32 = jnp.float32

Y_HI, Z_QUAD, Z_PAIR, CORES = 4, 4, 2, 2
AXES = ("y_lo", "x", "y_hi", "z_quad", "z_pair", "core")
FSDP = ("y_lo", "x")

HEAD_SETS = ((1, 2, 5, 6), (0, 3, 4, 7))


def rank_of(shard, core):
    return 2 * (3 - shard // 2) + shard % 2 if core else shard


def block_tables():
    sends = np.zeros((8, 2, 2), np.int32)
    orders = np.zeros((2, 2, 16), np.int32)
    for half, heads in enumerate(HEAD_SETS):
        for shard in range(8):
            picked = [k for k in range(3) if (3 * shard + k) % 8 in heads] + ([3] if shard in heads else [])
            assert len(picked) == 2
            for place, k in enumerate(picked):
                sends[shard, half, place] = k
                kind, m = (3, shard) if k == 3 else divmod(3 * shard + k, 8)
                for core in range(2):
                    listed = heads[::-1] if core else heads
                    orders[half, core, 4 * kind + listed.index(m)] = 2 * rank_of(shard, core) + place
    return sends.reshape(-1), orders.reshape(-1)


SENDS, ORDERS = block_tables()


def owns(x, half):
    return int(x in (0, 3)) == half


CORE_SWAP = [(0, 1), (1, 0)]
PAIR_SWAP = [(0, 1), (1, 0)]
TO_OWNER = [
    (2 * x + half, 2 * x + (1 - half) if owns(x, half) else 2 * (x ^ 1) + half) for x in range(4) for half in range(2)
]
ACROSS = [(2 * x + half, 2 * (x ^ 1) + (1 - half)) for x in range(4) for half in range(2) if not owns(x, half)]


SHARDS = ("y_lo", "x", "core")
SHARD_GROUPS = [[rank_of(rank, core) * CORES + core for rank in range(8)] for core in range(CORES)]
CROSS = ("y_lo", "y_hi", "z_quad", "z_pair", "core")


def cross_groups(first):
    def place(y_lo, y, z, half, core):
        return (((y_lo * Y_HI + y % Y_HI) * Z_QUAD + z % Z_QUAD) * Z_PAIR + half) * CORES + core

    groups = []
    for y_lo in range(2):
        for half in range(Z_PAIR):
            for other in range(4):
                groups.append([place(y_lo, other, z + 2 * half, half, first) for z in range(Z_QUAD)])
                groups.append([place(y_lo, y + 2 * y_lo, other, half, 1 - first) for y in range(Y_HI)])
    return groups


def half_of(place_ref):
    return place_ref[0] // CORES % Z_PAIR


def front_kernel(
    place_ref,
    sends_ref,
    count_ref,
    patches_ref,
    gain_ref,
    images_ref,
    qkv_ref,
    proj_ref,
    out_ref,
    blocks_ref,
    rows_ref,
    message_ref,
    held_ref,
    read_sems,
    write_sems,
    sems,
):
    shard = place_ref[0] // (Y_HI * Z_QUAD * Z_PAIR * CORES)
    core = place_ref[0] % CORES
    for i in range(2):
        choice = sends_ref[4 * shard + 2 * half_of(place_ref) + i]

        @pl.when(choice < 3)
        def _():
            pltpu.make_async_copy(qkv_ref.at[2 * jnp.minimum(choice, 2) + core], held_ref.at[i], read_sems.at[i]).start()

        @pl.when(choice == 3)
        def _():
            pltpu.make_async_copy(proj_ref.at[core], held_ref.at[i], read_sems.at[i]).start()

    fetch = pltpu.make_async_copy(patches_ref, rows_ref, sems.at[0])
    fetch.start()
    copies = []
    for i in range(2):
        pltpu.make_async_copy(proj_ref.at[0], held_ref.at[i], read_sems.at[i]).wait()
        for peer in range(8):
            copies.append(pltpu.make_async_copy(held_ref.at[i], blocks_ref.at[peer, i], write_sems.at[8 * i + peer]))
            copies[-1].start()

    fetch.wait()
    inputs = rows_ref[...].astype(F32)
    row_mean = jnp.mean(inputs, axis=1, keepdims=True)
    centred = inputs - row_mean
    variance = jnp.mean(centred * centred, axis=1, keepdims=True)
    message_ref[:ROWS, :] = (centred * lax.rsqrt(variance + EPSILON) * gain_ref[...].reshape(1, WIDTH)).astype(BF16)
    dead = lax.broadcasted_iota(jnp.int32, (1, ROWS), 1) >= count_ref[0] * TILE
    code = (images_ref[...].reshape(1, ROWS) + jnp.where(dead, 64, 0)).astype(F32)
    message_ref[ROWS:, :] = jnp.zeros((NOTE, WIDTH), BF16)
    message_ref[ROWS:, :ROWS] = jnp.broadcast_to(code, (NOTE, ROWS)).astype(BF16)
    copies.append(pltpu.make_async_copy(message_ref, out_ref, sems.at[1]))
    copies[-1].start()
    for copy in copies:
        copy.wait()


def attention_kernel(
    place_ref,
    order_ref,
    x0_ref,
    x1_ref,
    x2_ref,
    x3_ref,
    blocks_ref,
    c0_ref,
    c1_ref,
    c2_ref,
    c3_ref,
    out_ref,
    grad_ref,
    x_ref,
    weight_ref,
    context_ref,
    c_ref,
    x_sems,
    sems,
    c_sems,
    out_sem,
):
    scale = HEAD**-0.5 * math.log2(math.e)
    hidden = -1e30 * HEAD**0.5
    copies = []
    for slot in range(12):
        source = blocks_ref.at[order_ref[16 * (place_ref[0] % 4) + slot]]
        copies.append(pltpu.make_async_copy(source, weight_ref.at[slot * HEAD : (slot + 1) * HEAD], sems.at[slot]))
    arrivals = [
        pltpu.make_async_copy(ref, x_ref.at[part], x_sems.at[part])
        for part, ref in enumerate((x0_ref, x1_ref, x2_ref, x3_ref))
    ]
    cotangents = [
        pltpu.make_async_copy(ref, c_ref.at[part * ROWS : (part + 1) * ROWS], c_sems.at[part])
        for part, ref in enumerate((c0_ref, c1_ref, c2_ref, c3_ref))
    ]
    for copy in copies + arrivals + cotangents:
        copy.start()
    for copy in copies + arrivals:
        copy.wait()
    everything = [
        lax.dot_general(
            weight_ref[...], x_ref[part, :ROWS, :], (((1,), (1,)), ((), ())), preferred_element_type=F32
        ).astype(BF16)
        for part in range(4)
    ]
    def piece(part, kind, head):
        return everything[part][(4 * kind + head) * HEAD : (4 * kind + head + 1) * HEAD, :]

    def products(part):
        return [
            lax.dot_general(
                piece(part, 1, head), piece(part, 0, head), (((0,), (0,)), ((), ())), preferred_element_type=F32
            )
            for head in range(4)
        ]

    scores = products(0)
    for part in range(4):
        following = products(part + 1) if part < 3 else None
        code = x_ref[part, ROWS:, :ROWS].astype(F32)[0:1, :]
        square = jnp.broadcast_to(code, (ROWS, ROWS))
        allowed = square == square.T
        alive = code < 64.0
        weights, totals = [], []
        for head in range(4):
            masked = jnp.where(allowed, scores[head], hidden)
            peak = jnp.max(masked, axis=0, keepdims=True)
            weight = jnp.exp2((masked - peak) * scale)
            totals.append(jnp.sum(weight, axis=0, keepdims=True))
            weights.append(weight.astype(BF16))
        for head in range(4):
            context = jnp.dot(piece(part, 2, head), weights[head], preferred_element_type=F32)
            context = jnp.where(alive, context / totals[head], 0.0)
            context_ref[head * HEAD : (head + 1) * HEAD, part * ROWS : (part + 1) * ROWS] = context.astype(BF16)
        scores = following
    store = pltpu.make_async_copy(context_ref, out_ref, out_sem)
    store.start()
    for copy in cotangents:
        copy.wait()
    for start in range(0, WIDTH, 256):
        columns = slice(start, start + 256)
        grad_ref[:, columns] = jnp.dot(
            context_ref[...], c_ref[:, columns], preferred_element_type=F32
        ).astype(BF16)
    store.wait()


def project_kernel(
    place_ref, order_ref, from_ref, blocks_ref, keep_ref, send_ref, context_ref, held_ref, weight_ref, sems, sem, out_sems
):
    copies = [pltpu.make_async_copy(from_ref, context_ref, sem)]
    copies[0].start()
    for slot in range(4):
        source = blocks_ref.at[order_ref[16 * (place_ref[0] % 4) + 12 + slot]]
        copies.append(pltpu.make_async_copy(source, weight_ref.at[slot * HEAD : (slot + 1) * HEAD], sems.at[slot]))
        copies[-1].start()
    for copy in copies:
        copy.wait()
    stores = []
    for part in (1, 3, 0, 2):
        projected = lax.dot_general(
            context_ref[:, part * ROWS : (part + 1) * ROWS],
            weight_ref[...],
            (((0,), (0,)), ((), ())),
            preferred_element_type=F32,
        )
        held_ref[part] = projected.astype(BF16)
        target = send_ref if part % 2 else keep_ref
        stores.append(pltpu.make_async_copy(held_ref.at[part], target.at[part // 2], out_sems.at[part]))
        stores[-1].start()
    for store in stores:
        store.wait()


def sum_kernel(terms_ref, copies_ref):
    total = terms_ref[0].astype(F32)
    for i in range(1, terms_ref.shape[0]):
        total = total + terms_ref[i].astype(F32)
    total = total.astype(BF16)
    for i in range(copies_ref.shape[0]):
        copies_ref[i] = total


VMEM = pl.BlockSpec(memory_space=pltpu.VMEM)
SMEM = pl.BlockSpec(memory_space=pltpu.SMEM)
HBM = pl.BlockSpec(memory_space=pltpu.HBM)
DMA = pltpu.SemaphoreType.DMA


def call(kernel, out_shape, in_specs, out_specs, scratch=(), limit=60 << 20, flops=0, read=0):
    return pl.pallas_call(
        kernel,
        out_shape=out_shape,
        in_specs=in_specs,
        out_specs=out_specs,
        scratch_shapes=scratch,
        compiler_params=pltpu.CompilerParams(vmem_limit_bytes=limit),
        cost_estimate=pl.CostEstimate(flops=flops, bytes_accessed=read, transcendentals=0),
    )


def array(*shape):
    return jax.ShapeDtypeStruct(shape, BF16)


def sum_of(terms, copies):
    return call(
        sum_kernel,
        array(copies, *terms.shape[1:]),
        [VMEM],
        VMEM,
        limit=16 << 20,
        read=2 * (copies + terms.shape[0]) * 40 * WIDTH
    )(terms)


def shards(patches, ln_gain, qkv_weight, proj_weight, out_cotangent, tile_counts, segment_ids):
    core = lax.axis_index("core")
    half = lax.axis_index("z_pair")
    x = lax.axis_index("x")
    shard = lax.axis_index("y_lo") * 4 + x
    place = lax.axis_index(AXES).reshape(1)
    sends, orders = jnp.asarray(SENDS), jnp.asarray(ORDERS)

    def to_core(value):
        return lax.ppermute(value, "core", CORE_SWAP)

    def to_pair(value):
        return lax.ppermute(value, "z_pair", PAIR_SWAP)

    message, own = call(
        front_kernel,
        (array(ROWS + NOTE, WIDTH), array(8, 2, HEAD, WIDTH)),
        [SMEM, SMEM, SMEM, HBM, VMEM, VMEM, HBM, HBM],
        (HBM, HBM),
        [
            pltpu.VMEM((ROWS, WIDTH), BF16),
            pltpu.VMEM((ROWS + NOTE, WIDTH), BF16),
            pltpu.VMEM((2, HEAD, WIDTH), BF16),
            DMA((2,)),
            DMA((16,)),
            DMA((2,)),
        ],
        read=6 << 20,
    )(
        place,
        sends,
        tile_counts,
        patches,
        ln_gain,
        segment_ids,
        qkv_weight.T.reshape(6, HEAD, WIDTH),
        proj_weight.reshape(2, HEAD, WIDTH),
    )
    blocks = lax.all_to_all(own, SHARDS, 0, 0, axis_index_groups=SHARD_GROUPS).reshape(16, HEAD, WIDTH)

    message_pair = to_pair(message)
    cotangent_pair = to_pair(out_cotangent)
    message_core = to_core(message)
    cotangent_core = to_core(out_cotangent)
    message_both = to_core(message_pair)
    cotangent_both = to_core(cotangent_pair)

    context, grad = call(
        attention_kernel,
        (array(4 * HEAD, 4 * ROWS), array(4 * HEAD, WIDTH)),
        [SMEM, SMEM] + [HBM] * 9,
        (HBM, VMEM),
        [
            pltpu.VMEM((4, ROWS + NOTE, WIDTH), BF16),
            pltpu.VMEM((12 * HEAD, WIDTH), BF16),
            pltpu.VMEM((4 * HEAD, 4 * ROWS), BF16),
            pltpu.VMEM((4 * ROWS, WIDTH), BF16),
            DMA((4,)),
            DMA((12,)),
            DMA((4,)),
            DMA,
        ],
        limit=52 << 20,
        flops=2 * 1024 * 1280 * 1280 + 4 * 16 * 256 * 256 * 128,
        read=12 << 20,
    )(
        place,
        orders,
        message,
        message_core,
        message_pair,
        message_both,
        blocks,
        out_cotangent,
        cotangent_core,
        cotangent_pair,
        cotangent_both,
    )

    keep_out, send_out = call(
        project_kernel,
        (array(2, ROWS, WIDTH), array(2, ROWS, WIDTH)),
        [SMEM, SMEM, HBM, HBM],
        (HBM, HBM),
        [
            pltpu.VMEM((4 * HEAD, 4 * ROWS), BF16),
            pltpu.VMEM((4, ROWS, WIDTH), BF16),
            pltpu.VMEM((4 * HEAD, WIDTH), BF16),
            DMA((4,)),
            DMA,
            DMA((4,)),
        ],
        limit=52 << 20,
        flops=2 * 1024 * 1280 * 320,
        read=6 << 20,
    )(place, orders, context, blocks)

    grad = lax.all_to_all(grad.reshape(8, 40, WIDTH), SHARDS, 0, 0, axis_index_groups=SHARD_GROUPS)
    grad, keep_late = lax.optimization_barrier((grad, keep_out))
    grad = sum_of(grad, Z_QUAD)
    from_core = to_core(send_out)
    for_pair = (keep_out[1].astype(F32) + from_core[1].astype(F32)).astype(BF16)
    grad = lax.all_to_all(grad, CROSS, 0, 0, axis_index_groups=cross_groups(0))
    grad, from_core_late = lax.optimization_barrier((grad, from_core))
    grad = sum_of(grad, Y_HI)
    from_pair = to_pair(for_pair)
    grad = lax.all_to_all(grad, CROSS, 0, 0, axis_index_groups=cross_groups(1))
    grad, from_pair = lax.optimization_barrier((grad, from_pair))
    grad = sum_of(grad, 1)[0]

    first = lax.ppermute(grad, ("x", "z_pair"), TO_OWNER)
    second = lax.ppermute(grad, ("x", "z_pair"), ACROSS)
    projected = keep_late[0].astype(F32) + from_core_late[0].astype(F32) + from_pair.astype(F32)
    alive = lax.iota(jnp.int32, ROWS) < tile_counts[0] * TILE
    output = jnp.where(alive[:, None], patches.astype(F32) + projected, F32(0.0)).astype(BF16)
    second, output = lax.optimization_barrier((second, output))
    owner = ((x == 0) | (x == 3)) == (half == 1)
    two = lax.broadcasted_iota(jnp.int32, (2, 1, 1), 0)
    head_grad = jnp.where(two == x % 2, jnp.where(owner, grad, first), jnp.where(owner, first, second))
    head_grad = head_grad.reshape(HEAD, WIDTH)
    proj_grad = jnp.where(two == core, head_grad, to_core(head_grad)).reshape(2 * HEAD, WIDTH)
    return output, proj_grad


def solution(mesh):
    fine = Mesh(mesh.devices.reshape(2, 4, Y_HI, Z_QUAD, Z_PAIR, CORES), AXES)
    return jax.shard_map(
        shards,
        mesh=fine,
        in_specs=(P(AXES, None), P(), P(None, FSDP), P(FSDP, None), P(AXES, None), P(AXES), P(AXES)),
        out_specs=(P(AXES, None), P(FSDP, None)),
        check_vma=False,
    )
```
